256 devices in a mesh: edp: 16 (over z_lo, x, core), ep: 16 (over z_hi, y).
Axes of the slice: x: 4, y: 4, z: 8 (z_hi: 4, z_lo: 2; z = z_hi * 2 + z_lo), core: 2. Of those that a mesh axis runs over, the one named last changes fastest.
Arguments:
- tokens: bfloat16 [32768, 5120], P(('edp', 'ep')), may hold values from -6 to 6
- cotangent: bfloat16 [32768, 5120], P(('edp', 'ep')), may hold values from -4 to 4
- gate_probs: bfloat16 [32768, 6], P(('edp', 'ep')), may hold values from 0.099609375 to 1
- expert_ids: int32 [32768, 6], P(('edp', 'ep')), may hold values from 0 to 159, all different within a row
- w_gate: bfloat16 [16, 1536, 5120], P('ep', 'edp'), may hold values from -0.078125 to 0.078125
- w_up: bfloat16 [16, 1536, 5120], P('ep', 'edp'), may hold values from -0.078125 to 0.078125
- w_down: bfloat16 [16, 1536, 5120], P('ep', 'edp'), may hold values from -0.15625 to 0.15625
Outputs:
- token_grad: bfloat16 [32768, 5120], P(('edp', 'ep'))
- gate_grad: bfloat16 [32768, 6], P(('edp', 'ep'))
- gate_wgrad: bfloat16 [16, 1536, 5120], P('ep', 'edp')
- up_wgrad: bfloat16 [16, 1536, 5120], P('ep', 'edp')
- down_wgrad: bfloat16 [16, 1536, 5120], P('ep', 'edp')
The draws below stay inside these ranges and needn't reach their ends.
Inputs may be any that keep to these rules, and one draw needn't show every extreme that they name: `expert_ids`: each row holds 6 different ids, and every id appears in some row.
All inputs are finite; a program needn't handle non-finite values.
Results may differ from the reference program's by a relative error of at most 0.008.
Values may be sent and summed in bfloat16 or wider, within the bound.
No kernel may reach another device: no remote copies, remote signals or barrier semaphores. Data moves between devices by JAX's collectives and lax.ppermute only.
A program may use at most 128 MiB of HBM per device.

```python
import math
import jax
import jax.numpy as jnp
from jax import lax

D = 5120
H = 1536
ALL_EXPERTS = 160
TOP = 6
EXP_EP = 1
TOK_DEV = 128
EXPERTS = 16
SPLIT = 16
CAP = 3
TOKENS = 32768
N_EDP = 16
N_EP = 16


def block_levels(rng, extent, cuts, smallest, largest):
    gain = 1.0
    for position, shards_of in cuts:
        steps = jax.random.uniform(jax.random.fold_in(jax.random.fold_in(rng, 6), position), (shards_of,), jnp.float32, smallest / len(cuts), largest / len(cuts))
        gain = gain * jnp.repeat(jnp.exp(steps), extent[position] // shards_of).reshape((-1,) + (1,) * (len(extent) - 1 - position))
    return gain


def picks_of(key, rows, count, top, lift):
    ranking = jax.random.permutation(jax.random.fold_in(key, 1), count)
    pull = ranking
    for power in range(3):
        pull = pull * pull // count
    pull = pull * lift // count
    chance = jax.random.randint(jax.random.fold_in(key, 2), (rows, count), 0, 4096) + pull
    sure = jax.random.permutation(jax.random.fold_in(key, 3), rows)[jnp.arange(count) % rows]
    chance = jnp.where(jnp.arange(rows)[:, None] == sure[None, :], 1 << 14, chance)
    merit = chance * count + jnp.arange(count)
    return lax.top_k(merit.astype(jnp.int32), top)[1].astype(jnp.int32)


def centred(rng, shape, width, most, shards=(), kind=jnp.bfloat16):
    level = block_levels(rng, shape, shards, -0.22, 0.18) if shards else 1.0
    array = jax.random.normal(rng, shape, jnp.float32) * width * level
    return jnp.minimum(jnp.maximum(array, -most), most).astype(kind)


def setup_inputs(seed: int = 0) -> dict:
    key_list = jax.random.split(jax.random.key(seed), 8)
    return {
        "tokens": centred(key_list[0], (TOKENS, D), 1.0, 6.0, ((0, 256),)),
        "cotangent": centred(key_list[1], (TOKENS, D), 0.5, 4.0, ((0, 256),)),
        "gate_probs": jnp.clip(jnp.exp(math.log(1.0) - 2.306499 * jax.random.uniform(key_list[2], (TOKENS, TOP), jnp.float32) ** block_levels(key_list[2], (TOKENS, TOP), ((0, 256),), -0.2, 0.2)), 0.099609375, 1.0).astype(jnp.bfloat16),
        "expert_ids": picks_of(key_list[3], TOKENS, ALL_EXPERTS, TOP, 614),
        "w_gate": centred(key_list[4], (N_EP, EXP_EP * H, D), D ** -0.5, 0.078125, ((0, 16), (1, 16))),
        "w_up": centred(key_list[5], (N_EP, EXP_EP * H, D), D ** -0.5, 0.078125, ((0, 16), (1, 16))),
        "w_down": centred(key_list[6], (N_EP, EXP_EP * H, D), H ** -0.5, 0.15625, ((0, 16), (1, 16))),
    }


def route_tables(expert_ids, experts, capacity):
    tok_count = expert_ids.shape[0]
    matches = (expert_ids[:, :, None] == jnp.arange(experts, dtype=jnp.int32)[None, None, :]).astype(jnp.float32)
    counts = jnp.sum(matches, axis=1)
    positions = jnp.arange(tok_count, dtype=jnp.int32)
    earlier = (positions[None, :] < positions[:, None]).astype(jnp.float32)
    before = jnp.dot(earlier, counts, precision=lax.Precision.HIGHEST)
    slot_pos = jnp.sum(matches * before[:, None, :], axis=2)
    column = expert_ids.astype(jnp.float32) * capacity + slot_pos
    inside = (expert_ids < experts) & (slot_pos < capacity)
    targets = jnp.arange(experts * capacity, dtype=jnp.float32)
    hits = inside[:, :, None] & (column[:, :, None] == targets[None, None, :])
    return jnp.where(hits, 1.0, 0.0).astype(jnp.float32)


def expert_step(operands):
    rows_x, rows_dy, rows_p, gate_mat, up_mat, down_mat = operands
    contract = (((1,), (1,)), ((), ()))
    pre_gate = lax.dot_general(rows_x, gate_mat, contract, preferred_element_type=jnp.float32)
    pre_up = lax.dot_general(rows_x, up_mat, contract, preferred_element_type=jnp.float32)
    sigma_gate = jax.nn.sigmoid(pre_gate)
    hidden = pre_gate * sigma_gate * pre_up
    back_hid = lax.dot_general(rows_dy, down_mat, contract, preferred_element_type=jnp.float32)
    slot_dp = jnp.sum(hidden * back_hid, axis=1)
    prob_col = rows_p.astype(jnp.float32)[:, None]
    grad_hid = prob_col * back_hid
    grad_gate = (grad_hid * pre_up * sigma_gate * (1.0 + pre_gate * (1.0 - sigma_gate))).astype(jnp.bfloat16)
    grad_up = (grad_hid * pre_gate * sigma_gate).astype(jnp.bfloat16)
    scaled_cot = (prob_col * rows_dy.astype(jnp.float32)).astype(jnp.bfloat16)
    hidden_half = hidden.astype(jnp.bfloat16)
    outer = (((0,), (0,)), ((), ()))
    down_grad = lax.dot_general(hidden_half, scaled_cot, outer, preferred_element_type=jnp.float32).astype(jnp.bfloat16)
    gate_grad = lax.dot_general(grad_gate, rows_x, outer, preferred_element_type=jnp.float32).astype(jnp.bfloat16)
    up_grad = lax.dot_general(grad_up, rows_x, outer, preferred_element_type=jnp.float32).astype(jnp.bfloat16)
    slice_width = H // SPLIT
    row_total = rows_x.shape[0]
    gate_slices = grad_gate.reshape(row_total, SPLIT, slice_width).transpose(1, 0, 2)
    up_slices = grad_up.reshape(row_total, SPLIT, slice_width).transpose(1, 0, 2)
    gate_blocks = gate_mat.reshape(SPLIT, slice_width, D)
    up_blocks = up_mat.reshape(SPLIT, slice_width, D)

    def add_slice(running, pieces):
        left_gate, left_up, right_gate, right_up = pieces
        partial_sum = jnp.dot(left_gate, right_gate, preferred_element_type=jnp.float32)
        partial_sum = partial_sum + jnp.dot(left_up, right_up, preferred_element_type=jnp.float32)
        rounded = lax.optimization_barrier(partial_sum.astype(jnp.bfloat16))
        return running + rounded.astype(jnp.float32), None

    start_sum = jnp.zeros((row_total, D), jnp.float32)
    slot_dx, unused = lax.scan(add_slice, start_sum, (gate_slices, up_slices, gate_blocks, up_blocks))
    return slot_dx.astype(jnp.bfloat16), slot_dp.astype(jnp.bfloat16), gate_grad, up_grad, down_grad


def reference(tokens, cotangent, gate_probs, expert_ids, w_gate, w_up, w_down):
    blocks = N_EDP * N_EP
    experts = EXPERTS
    tok_blocks = tokens.reshape(blocks, TOK_DEV, D)
    cot_blocks = cotangent.reshape(blocks, TOK_DEV, D)
    prob_blocks = gate_probs.reshape(blocks, TOK_DEV, TOP).astype(jnp.float32)
    id_blocks = expert_ids.reshape(blocks, TOK_DEV, TOP)
    tables = jax.vmap(lambda ids: route_tables(ids, experts, CAP))(id_blocks)
    route_matrix = jnp.sum(tables, axis=2)
    sent_x = jnp.einsum('btc,btd->bcd', route_matrix, tok_blocks.astype(jnp.float32)).astype(jnp.bfloat16)
    sent_dy = jnp.einsum('btc,btd->bcd', route_matrix, cot_blocks.astype(jnp.float32)).astype(jnp.bfloat16)
    sent_p = jnp.einsum('btrc,btr->bc', tables, prob_blocks).astype(jnp.bfloat16)
    rows_x = sent_x.reshape(blocks, experts, CAP, D).transpose(1, 0, 2, 3).reshape(experts, blocks * CAP, D)
    rows_dy = sent_dy.reshape(blocks, experts, CAP, D).transpose(1, 0, 2, 3).reshape(experts, blocks * CAP, D)
    rows_p = sent_p.reshape(blocks, experts, CAP).transpose(1, 0, 2).reshape(experts, blocks * CAP)
    gate_all = w_gate.reshape(experts, H, D)
    up_all = w_up.reshape(experts, H, D)
    down_all = w_down.reshape(experts, H, D)
    slot_dx, slot_gp, gate_wgrad, up_wgrad, down_wgrad = lax.map(
        expert_step, (rows_x, rows_dy, rows_p, gate_all, up_all, down_all))
    back_x = slot_dx.reshape(experts, blocks, CAP, D).transpose(1, 0, 2, 3).reshape(blocks, experts * CAP, D)
    back_p = slot_gp.reshape(experts, blocks, CAP).transpose(1, 0, 2).reshape(blocks, experts * CAP)
    token_grad = jnp.einsum('btc,bcd->btd', route_matrix, back_x.astype(jnp.float32)).astype(jnp.bfloat16)
    gate_grad = jnp.einsum('btrc,bc->btr', tables, back_p.astype(jnp.float32)).astype(jnp.bfloat16)
    shape_out = (N_EP, EXP_EP * H, D)
    return (token_grad.reshape(TOKENS, D), gate_grad.reshape(TOKENS, TOP),
            gate_wgrad.reshape(shape_out), up_wgrad.reshape(shape_out), down_wgrad.reshape(shape_out))
```

```python
import jax
import jax.numpy as jnp
from jax import lax
from jax.sharding import PartitionSpec as P

CAP = 3
XN = 4


def x_perm(step):
    pairs = []
    for i in range(16):
        z, x, c = i >> 3, (i >> 1) & 3, i & 1
        pairs.append((i, z * 8 + ((x + step) % XN) * 2 + c))
    return pairs


X_UP = x_perm(1)
X_DOWN = x_perm(-1)
Z_SWAP = [(i, i ^ 8) for i in range(16)]
C_SWAP = [(i, i ^ 1) for i in range(16)]


def send(a, perm):
    return lax.ppermute(a, "edp", perm)


def route_tables(expert_ids, experts, capacity):
    tok_count = expert_ids.shape[0]
    matches = (
        expert_ids[:, :, None] == jnp.arange(experts, dtype=jnp.int32)[None, None, :]
    ).astype(jnp.float32)
    counts = jnp.sum(matches, axis=1)
    positions = jnp.arange(tok_count, dtype=jnp.int32)
    earlier = (positions[None, :] < positions[:, None]).astype(jnp.float32)
    before = jnp.dot(earlier, counts, precision=lax.Precision.HIGHEST)
    slot_pos = jnp.sum(matches * before[:, None, :], axis=2)
    column = expert_ids.astype(jnp.float32) * capacity + slot_pos
    inside = (expert_ids < experts) & (slot_pos < capacity)
    targets = jnp.arange(experts * capacity, dtype=jnp.float32)
    hits = inside[:, :, None] & (column[:, :, None] == targets[None, None, :])
    return jnp.where(hits, 1.0, 0.0).astype(jnp.float32)


def gather_chips(a):
    other = send(a, Z_SWAP)
    left = send(a, X_UP)
    right = send(a, X_DOWN)
    o_left = send(other, X_UP)
    o_right = send(other, X_DOWN)
    far = send(left, X_UP)
    o_far = send(o_right, X_DOWN)
    return [a, left, far, right, other, o_left, o_far, o_right]


def add(*parts):
    total = parts[0].astype(jnp.float32)
    for p in parts[1:]:
        total = total + p.astype(jnp.float32)
    return total


def scatter_chips(parts, join):
    own, left, far, right, other, o_left, o_far, o_right = parts
    of = send(o_far, X_UP)
    ol = send(o_left, X_DOWN)
    f = send(far, X_DOWN)
    r = send(right, X_UP)
    o_r = send(join(o_right, of), X_UP)
    l = send(join(left, f), X_DOWN)
    oz = send(join(other, ol, o_r), Z_SWAP)
    return join(own, r, l, oz)


def per_device(tokens, cotangent, gate_probs, expert_ids, w_gate, w_up, w_down):
    ep_size = lax.axis_size("ep")
    experts = ep_size
    width = tokens.shape[1]
    capacity = CAP
    rows = experts * capacity
    gate_mat, up_mat, down_mat = w_gate[0], w_up[0], w_down[0]
    gate_2, up_2, down_2 = (send(w, C_SWAP) for w in (gate_mat, up_mat, down_mat))
    tables = route_tables(expert_ids, experts, capacity)
    route_matrix = jnp.sum(tables, axis=1).astype(jnp.bfloat16)
    send_x = jnp.einsum("tc,td->cd", route_matrix, tokens, preferred_element_type=jnp.float32)
    send_x = send_x.astype(jnp.bfloat16).reshape(ep_size, capacity, width)
    send_dy = jnp.einsum("tc,td->cd", route_matrix, cotangent, preferred_element_type=jnp.float32)
    send_p = jnp.einsum("trc,tr->c", tables, gate_probs.astype(jnp.float32))
    send_dy = jnp.concatenate(
        [send_dy, jnp.broadcast_to(send_p[:, None], (rows, 128))], axis=1
    ).astype(jnp.bfloat16)
    send_dy = send_dy.reshape(ep_size, capacity, width + 128)
    recv_x = lax.all_to_all(send_x, "ep", split_axis=0, concat_axis=0, tiled=True)
    recv_dy = lax.all_to_all(send_dy, "ep", split_axis=0, concat_axis=0, tiled=True)
    x_parts = gather_chips(recv_x.reshape(rows, width))
    dy_parts = gather_chips(recv_dy.reshape(rows, width + 128))
    x_rows = jnp.concatenate(x_parts, axis=0)
    dy_ext = jnp.concatenate(dy_parts, axis=0)
    dy_rows = dy_ext[:, :width]
    prob_col = dy_ext[:, width : width + 1].astype(jnp.float32)
    gate_all = jnp.concatenate([gate_mat, gate_2], axis=0)
    up_all = jnp.concatenate([up_mat, up_2], axis=0)
    down_all = jnp.concatenate([down_mat, down_2], axis=0)
    contract = (((1,), (1,)), ((), ()))
    pre_gate = lax.dot_general(x_rows, gate_all, contract, preferred_element_type=jnp.float32)
    pre_up = lax.dot_general(x_rows, up_all, contract, preferred_element_type=jnp.float32)
    sigma_gate = jax.nn.sigmoid(pre_gate)
    hidden = pre_gate * sigma_gate * pre_up
    back_hid = lax.dot_general(dy_rows, down_all, contract, preferred_element_type=jnp.float32)
    slot_part = jnp.sum(hidden * back_hid, axis=1, keepdims=True)
    grad_hid = prob_col * back_hid
    grad_gate = (grad_hid * pre_up * sigma_gate * (1.0 + pre_gate * (1.0 - sigma_gate))).astype(
        jnp.bfloat16
    )
    grad_up = (grad_hid * pre_gate * sigma_gate).astype(jnp.bfloat16)
    scaled_cot = (prob_col * dy_rows.astype(jnp.float32)).astype(jnp.bfloat16)
    hidden_half = hidden.astype(jnp.bfloat16)
    partial_sum = jnp.dot(
        jnp.concatenate([grad_gate, grad_up], axis=1),
        jnp.concatenate([gate_all, up_all], axis=0),
        preferred_element_type=jnp.float32,
    )

    def pack(total, dp):
        high = dp.astype(jnp.bfloat16)
        low = (dp - high.astype(jnp.float32)).astype(jnp.bfloat16)
        return jnp.concatenate(
            [
                total.astype(jnp.bfloat16),
                jnp.broadcast_to(high, (dp.shape[0], 64)),
                jnp.broadcast_to(low, (dp.shape[0], 64)),
            ],
            axis=1,
        )

    def join(*parts):
        total = add(*parts)
        dp = total[:, width : width + 1] + total[:, width + 64 : width + 65]
        return pack(total[:, :width], dp)

    packed = pack(partial_sum, slot_part)
    slot_sum = scatter_chips([packed[k * rows : (k + 1) * rows] for k in range(8)], join)
    outer = (((0,), (0,)), ((), ()))

    def wgrad(left, right):
        half = left.shape[1] // 2
        away = lax.dot_general(left[:, half:], right, outer, preferred_element_type=jnp.float32)
        came = send(away.astype(jnp.bfloat16), C_SWAP)
        mine = lax.dot_general(left[:, :half], right, outer, preferred_element_type=jnp.float32)
        return (mine + came.astype(jnp.float32)).astype(jnp.bfloat16)

    down_wgrad = wgrad(hidden_half, scaled_cot)
    gate_wgrad = wgrad(grad_gate, x_rows)
    up_wgrad = wgrad(grad_up, x_rows)

    slot_gp = slot_sum[:, width : width + 1].astype(jnp.float32) + slot_sum[
        :, width + 64 : width + 65
    ].astype(jnp.float32)
    slot_out = jnp.concatenate(
        [slot_sum[:, :width], jnp.broadcast_to(slot_gp, (rows, 128)).astype(jnp.bfloat16)], axis=1
    )
    back = lax.all_to_all(
        slot_out.reshape(ep_size, capacity, width + 128),
        "ep",
        split_axis=0,
        concat_axis=0,
        tiled=True,
    ).reshape(rows, width + 128)
    token_grad = jnp.dot(
        route_matrix, back[:, :width], preferred_element_type=jnp.float32
    ).astype(jnp.bfloat16)
    gate_grad = jnp.einsum("trc,c->tr", tables, back[:, width].astype(jnp.float32)).astype(
        jnp.bfloat16
    )
    return (token_grad, gate_grad, gate_wgrad[None], up_wgrad[None], down_wgrad[None])


def solution(mesh):
    tok = P(("edp", "ep"), None)
    wgt = P("ep", "edp", None)
    return jax.shard_map(
        per_device,
        mesh=mesh,
        in_specs=(tok, tok, tok, tok, wgt, wgt, wgt),
        out_specs=(tok, tok, wgt, wgt, wgt),
        check_vma=False,
    )
```

```python
import functools

import jax
import jax.numpy as jnp
from jax import lax
from jax.experimental import pallas as pl
from jax.experimental.pallas import tpu as pltpu
from jax.sharding import PartitionSpec as P

CAP = 3
QN = 8
LANES = 128
F32 = jnp.float32
BF16 = jnp.bfloat16


def x_perm(step):
    pairs = []
    for i in range(16):
        z, x, c = i >> 3, (i >> 1) & 3, i & 1
        pairs.append((i, z * 8 + ((x + step) % 4) * 2 + c))
    return pairs


X_UP = x_perm(1)
X_DOWN = x_perm(-1)
Z_SWAP = [(i, i ^ 8) for i in range(16)]
C_SWAP = [(i, i ^ 1) for i in range(16)]


def hop(a, perm):
    return lax.ppermute(a, "edp", perm)


def iota(shape, dim):
    return lax.broadcasted_iota(jnp.int32, shape, dim)


def dot(a, b):
    return jnp.dot(a, b, preferred_element_type=F32)


def dot_nt(a, b):
    return lax.dot_general(a, b, (((1,), (1,)), ((), ())), preferred_element_type=F32)


def call(kernel, outs, name, scratch=(), specs=None, out_specs=None, cost=None, limit=48):
    one = pl.BlockSpec(memory_space=pltpu.VMEM)
    params = pltpu.CompilerParams(vmem_limit_bytes=limit * 1024 * 1024)

    def run(*args):
        return pl.pallas_call(
            kernel,
            out_shape=outs,
            in_specs=[one] * len(args) if specs is None else specs,
            out_specs=jax.tree.map(lambda _: one, outs) if out_specs is None else out_specs,
            scratch_shapes=scratch,
            compiler_params=params,
            name=name,
            cost_estimate=cost
            and pl.CostEstimate(flops=cost[0], bytes_accessed=cost[1], transcendentals=0),
        )(*args)

    return run


def live_tables(ids_t):
    tokens = ids_t.shape[1]
    expert = iota((LANES, tokens), 0) >> 3
    hits = jnp.zeros((LANES, tokens), F32)
    for r in range(ids_t.shape[0]):
        hits = hits + jnp.where(ids_t[r : r + 1, :] == expert, 1.0, 0.0)
    earlier = jnp.where(iota((tokens, tokens), 0) < iota((tokens, tokens), 1), 1.0, 0.0)
    before = dot(hits.astype(BF16), earlier.astype(BF16))
    return [jnp.where(before == s, hits, 0.0) for s in range(CAP)]


def send_kernel(*refs, with_p):
    if with_p:
        ids_ref, probs_ref, tok_ref, out_ref = refs
    else:
        ids_ref, tok_ref, out_ref = refs
    ids_t = ids_ref[...]
    group = tok_ref.shape[1] // QN
    live = live_tables(ids_t)
    q = iota(live[0].shape, 0) & (QN - 1)
    for s in range(CAP):
        total = jnp.zeros((LANES, group), F32)
        for k in range(QN):
            pick = jnp.where(q == k, live[s], 0.0).astype(BF16)
            total = total + dot(pick, tok_ref[:, k * group : (k + 1) * group])
        out_ref[:, s * group : (s + 1) * group] = total.astype(BF16)
    if with_p:
        expert = iota(live[0].shape, 0) >> 3
        probs = jnp.zeros(live[0].shape, F32)
        for r in range(ids_t.shape[0]):
            probs = probs + jnp.where(
                ids_t[r : r + 1, :] == expert, probs_ref[r : r + 1, :].astype(F32), 0.0
            )
        lane = iota((LANES, LANES), 1)
        tail = jnp.zeros((LANES, LANES), F32)
        for s in range(CAP):
            col = jnp.sum(live[s] * probs, axis=1, keepdims=True)
            tail = tail + jnp.where(lane == s, col, 0.0)
        out_ref[:, CAP * group :] = tail.astype(BF16)


def unpack_kernel(in_ref, out_ref, *, group):
    row, col = iota((LANES, LANES), 0), iota((LANES, LANES), 1)
    swap = jnp.where((row & 15) * QN + (row >> 4) == col, 1.0, 0.0).astype(BF16)
    for s in range(CAP):
        got = dot(swap, in_ref[:, s * group : (s + 1) * group]).astype(BF16)
        for k in range(QN):
            out_ref[s * 16 : (s + 1) * 16, k * group : (k + 1) * group] = got[
                k * 16 : (k + 1) * 16, :
            ]
    if out_ref.shape[1] > QN * group:
        tail = dot(swap, in_ref[:, CAP * group :])
        for s in range(CAP):
            out_ref[s * 16 : (s + 1) * 16, QN * group :] = jnp.broadcast_to(
                tail[0:16, s : s + 1], (16, LANES)
            ).astype(BF16)


def fetch(copies):
    for c in copies:
        c.start()
    for c in copies:
        c.wait()


def pre_kernel(*refs, chunks):
    xs, (g, u, away) = refs[:chunks], refs[chunks : chunks + 3]
    out_ref, x_all, w_all, sems = refs[chunks + 3 :]
    rows, hid = xs[0].shape[0], g.shape[0]
    copies = [
        (xs[k], x_all.at[pl.ds(k * rows, rows)]) for k in range(chunks)
    ] + [
        (g, w_all.at[pl.ds(0, hid)]),
        (away.at[pl.ds(0, hid)], w_all.at[pl.ds(hid, hid)]),
        (u, w_all.at[pl.ds(2 * hid, hid)]),
        (away.at[pl.ds(hid, hid)], w_all.at[pl.ds(3 * hid, hid)]),
    ]
    fetch([pltpu.make_async_copy(a, b, sems.at[i]) for i, (a, b) in enumerate(copies)])
    out_ref[...] = jnp.zeros(out_ref.shape, F32)
    step = 640

    def body(n, carry):
        cols = pl.ds(pl.multiple_of(n * step, step), step)
        out_ref[...] += dot_nt(w_all[:, cols], x_all[:, cols])
        return carry

    lax.fori_loop(0, x_all.shape[1] // step, body, 0)


def main_kernel(*refs, chunks):
    ys, (g, u, d, away, pre_ref) = refs[:chunks], refs[chunks : chunks + 5]
    outs = refs[chunks + 5 : 2 * chunks + 5]
    mine_ref, away_ref, hid_ref, y_all, w_all, d_all, acc, sems = refs[2 * chunks + 5 :]
    rows, hid = ys[0].shape[0], g.shape[0]
    width = g.shape[1]
    total = rows * chunks
    copies = [
        (d, d_all.at[pl.ds(0, hid)]),
        (away.at[pl.ds(2 * hid, hid)], d_all.at[pl.ds(hid, hid)]),
    ] + [
        (ys[k], y_all.at[pl.ds(k * rows, rows)]) for k in range(chunks)
    ]
    late = [
        (g, w_all.at[pl.ds(0, hid)]),
        (away.at[pl.ds(0, hid)], w_all.at[pl.ds(hid, hid)]),
        (u, w_all.at[pl.ds(2 * hid, hid)]),
        (away.at[pl.ds(hid, hid)], w_all.at[pl.ds(3 * hid, hid)]),
    ]
    started = [
        pltpu.make_async_copy(a, b, sems.at[i]) for i, (a, b) in enumerate(copies + late)
    ]
    for c in started:
        c.start()
    for c in started[: len(copies)]:
        c.wait()
    acc[...] = jnp.zeros(acc.shape, F32)
    step = 640

    def body(n, carry):
        cols = pl.ds(pl.multiple_of(n * step, step), step)
        acc[...] += dot_nt(d_all[:, cols], y_all[:, cols])
        return carry

    lax.fori_loop(0, width // step, body, 0)
    back = acc[...]
    prob = jnp.transpose(y_all[:, width:].astype(F32))[0:1, :]
    gate, up = pre_ref[0 : 2 * hid, :], pre_ref[2 * hid :, :]
    sig = jax.nn.sigmoid(gate)
    hidden = gate * sig * up
    part = jnp.sum(hidden * back, axis=0, keepdims=True)
    scaled = prob * back
    d_gate = scaled * up * sig * (1.0 + gate * (1.0 - sig))
    d_up = scaled * gate * sig
    hid_ref[...] = hidden.astype(BF16)
    d_gate_h, d_up_h = d_gate.astype(BF16), d_up.astype(BF16)
    mine_ref[0:hid, :] = d_gate_h[0:hid, :]
    mine_ref[hid:, :] = d_up_h[0:hid, :]
    away_ref[0:hid, :] = d_gate_h[hid:, :]
    away_ref[hid:, :] = d_up_h[hid:, :]
    both = jnp.concatenate([jnp.transpose(d_gate), jnp.transpose(d_up)], axis=1).astype(BF16)
    high = part.astype(BF16).astype(F32)
    low = part - high
    tail = jnp.where(
        iota((LANES, total), 0) < LANES // 2,
        jnp.broadcast_to(high, (LANES, total)),
        jnp.broadcast_to(low, (LANES, total)),
    )
    tail = jnp.transpose(tail).astype(BF16)
    for k in range(chunks):
        outs[k][:, width:] = tail[k * rows : (k + 1) * rows, :]
    for c in started[len(copies) :]:
        c.wait()

    def body2(n, carry):
        cols = pl.ds(pl.multiple_of(n * step, step), step)
        got = dot(both, w_all[:, cols]).astype(BF16)
        for k in range(chunks):
            outs[k][:, cols] = got[k * rows : (k + 1) * rows, :]
        return carry

    lax.fori_loop(0, width // step, body2, 0)


def summed(refs):
    total = refs[0][...].astype(F32)
    for r in refs[1:]:
        total = total + r[...].astype(F32)
    return total


def join_kernel(*refs, width):
    *parts, out_ref = refs
    body = [p.at[:, pl.ds(0, width)] for p in parts]
    out_ref[:, 0:width] = summed(body).astype(BF16)
    tail = summed([p.at[:, pl.ds(width, LANES)] for p in parts])
    value = tail[:, 0:1] + tail[:, LANES // 2 : LANES // 2 + 1]
    high = value.astype(BF16).astype(F32)
    out_ref[:, width:] = jnp.where(
        iota(tail.shape, 1) < LANES // 2, high, value - high
    ).astype(BF16)


def last_kernel(*refs, group):
    *parts, out_ref = refs
    width = QN * group
    row, col = iota((LANES, LANES), 0), iota((LANES, LANES), 1)
    swap = jnp.where((col & 15) * QN + (col >> 4) == row, 1.0, 0.0).astype(BF16)
    total = summed([p.at[:, pl.ds(0, width)] for p in parts]).astype(BF16)
    for s in range(CAP):
        stack = jnp.concatenate(
            [total[s * 16 : (s + 1) * 16, k * group : (k + 1) * group] for k in range(QN)], axis=0
        )
        out_ref[:, s * group : (s + 1) * group] = dot(swap, stack).astype(BF16)
    tail = summed([p.at[:, pl.ds(width, LANES)] for p in parts])
    value = tail[:, 0:1] + tail[:, LANES // 2 : LANES // 2 + 1]
    lane = iota((16, LANES), 1)
    cols = jnp.zeros((16, LANES), F32)
    for s in range(CAP):
        cols = cols + jnp.where(lane == s, value[s * 16 : (s + 1) * 16, :], 0.0)
    stack = jnp.concatenate([cols] * QN, axis=0).astype(BF16)
    out_ref[:, CAP * group :] = dot(swap, stack).astype(BF16)


def wgrad_kernel(*refs, chunks, came):
    xs, ys = refs[:chunks], refs[chunks : 2 * chunks]
    rest = refs[2 * chunks :]
    if came:
        left_ref, hid_ref, came_ref, g_out, u_out, d_out, x_all, y_all, sems = rest
    else:
        left_ref, hid_ref, out_ref, x_all, y_all, sems = rest
    rows, width = xs[0].shape
    hid = left_ref.shape[0] // 2
    copies = [(xs[k], x_all.at[pl.ds(k * rows, rows)]) for k in range(chunks)]
    copies += [(ys[k], y_all.at[pl.ds(k * rows, rows)]) for k in range(chunks)]
    fetch([pltpu.make_async_copy(a, b, sems.at[i]) for i, (a, b) in enumerate(copies)])
    prob = y_all[:, width : width + 1].astype(F32)
    step = 640

    def body(n, carry):
        cols = pl.ds(pl.multiple_of(n * step, step), step)
        both = dot(left_ref[...], x_all[:, cols])
        scaled = (prob * y_all[:, cols].astype(F32)).astype(BF16)
        if came:
            down = dot(hid_ref[0:hid, :], scaled)
            g_out[:, cols] = (both[0:hid] + came_ref[0:hid, cols].astype(F32)).astype(BF16)
            u_out[:, cols] = (
                both[hid:] + came_ref[hid : 2 * hid, cols].astype(F32)
            ).astype(BF16)
            d_out[:, cols] = (down + came_ref[2 * hid :, cols].astype(F32)).astype(BF16)
        else:
            down = dot(hid_ref[hid:, :], scaled)
            out_ref[0 : 2 * hid, cols] = both.astype(BF16)
            out_ref[2 * hid :, cols] = down.astype(BF16)
        return carry

    lax.fori_loop(0, width // step, body, 0)


def final_kernel(ids_ref, in_ref, tok_ref, gate_ref, *, group):
    ids_t = ids_ref[...]
    live = live_tables(ids_t)
    lane = iota(live[0].shape, 1)
    sides = [jnp.transpose(v) for v in live]
    for k in range(QN):
        total = jnp.zeros((live[0].shape[1], group), F32)
        for s in range(CAP):
            pick = jnp.where((lane & (QN - 1)) == k, sides[s], 0.0).astype(BF16)
            total = total + dot(pick, in_ref[:, s * group : (s + 1) * group])
        tok_ref[:, k * group : (k + 1) * group] = total.astype(BF16)
    row = iota(live[0].shape, 0)
    value = jnp.zeros(live[0].shape, F32)
    for s in range(CAP):
        col = in_ref[:, CAP * group + s : CAP * group + s + 1].astype(F32)
        value = value + live[s] * col
    value = jnp.where((row & (QN - 1)) == 0, value, 0.0)
    for r in range(ids_t.shape[0]):
        mine = jnp.where(ids_t[r : r + 1, :] == (row >> 3), value, 0.0)
        gate_ref[r : r + 1, :] = jnp.sum(mine, axis=0, keepdims=True).astype(BF16)


def first_hops(a):
    return hop(a, Z_SWAP), hop(a, X_UP), hop(a, X_DOWN)


def gather_chips(a, other, left, right):
    o_left = hop(other, X_UP)
    o_right = hop(other, X_DOWN)
    far = hop(left, X_UP)
    o_far = hop(o_right, X_DOWN)
    return [a, left, far, right, other, o_left, o_far, o_right]


def per_device(tokens, cotangent, gate_probs, expert_ids, w_gate, w_up, w_down):
    width = tokens.shape[1]
    group = width // QN
    wide = width + LANES
    rows = CAP * 16
    total = 8 * rows
    g, u, d = w_gate[0], w_up[0], w_down[0]
    hid = g.shape[0]
    ids_t, probs_t = expert_ids.T, gate_probs.T
    shape = jax.ShapeDtypeStruct
    any_spec, vmem = pl.BlockSpec(memory_space=pl.ANY), pl.BlockSpec(memory_space=pltpu.VMEM)
    dma = pltpu.SemaphoreType.DMA

    def exchange(a):
        a = a.reshape(16, QN, a.shape[1])
        a = lax.all_to_all(a, "ep", split_axis=0, concat_axis=0, tiled=True)
        return a.reshape(LANES, a.shape[2])

    away_w = hop(jnp.concatenate([g, u, d], axis=0), C_SWAP)
    send_x = call(
        functools.partial(send_kernel, with_p=False),
        shape((LANES, CAP * group), BF16),
        "send_x",
        cost=(6 * 10**8, 2 * 10**6),
    )(ids_t, tokens)
    send_y = call(
        functools.partial(send_kernel, with_p=True),
        shape((LANES, CAP * group + LANES), BF16),
        "send_y",
        cost=(6 * 10**8, 2 * 10**6),
    )(ids_t, probs_t, cotangent)
    got_x = exchange(send_x)
    send_y, away_w, got_x = lax.optimization_barrier((send_y, away_w, got_x))
    x = call(
        functools.partial(unpack_kernel, group=group),
        shape((rows, width), BF16),
        "unpack_x",
        cost=(10**8, 10**6),
    )(got_x)
    first_x = first_hops(x)
    got_y, *first_x = lax.optimization_barrier((exchange(send_y), *first_x))
    xs = gather_chips(x, *first_x)
    y = call(
        functools.partial(unpack_kernel, group=group),
        shape((rows, wide), BF16),
        "unpack_y",
        cost=(10**8, 10**6),
    )(got_y)
    ys = gather_chips(y, *first_hops(y))
    pre = call(
        functools.partial(pre_kernel, chunks=8),
        shape((4 * hid, total), F32),
        "pre",
        scratch=[
            pltpu.VMEM((total, width), BF16),
            pltpu.VMEM((4 * hid, width), BF16),
            dma((12,)),
        ],
        specs=[any_spec] * 11,
        cost=(2 * total * width * 4 * hid, 8 * 10**6),
    )(*xs, g, u, away_w)
    *parts, mine, away, hidden = call(
        functools.partial(main_kernel, chunks=8),
        [shape((rows, wide), BF16)] * 8
        + [shape((2 * hid, total), BF16), shape((2 * hid, total), BF16), shape((2 * hid, total), BF16)],
        "main",
        scratch=[
            pltpu.VMEM((total, wide), BF16),
            pltpu.VMEM((4 * hid, width), BF16),
            pltpu.VMEM((2 * hid, width), BF16),
            pltpu.VMEM((2 * hid, total), F32),
            dma((14,)),
        ],
        specs=[any_spec] * 12 + [vmem],
        cost=(3 * total * width * 4 * hid, 14 * 10**6),
    )(*ys, g, u, d, away_w, pre)

    def join(*a):
        return call(
            functools.partial(join_kernel, width=width),
            shape((rows, wide), BF16),
            "join",
            cost=(10**6, 10**6),
        )(*a)

    own, left, far, right, other, o_left, o_far, o_right = parts
    of, ol = hop(o_far, X_UP), hop(o_left, X_DOWN)
    of, ol, far, away = lax.optimization_barrier((of, ol, far, away))
    o_r, f = hop(join(o_right, of), X_UP), hop(far, X_DOWN)
    scratch = [
        pltpu.VMEM((total, width), BF16),
        pltpu.VMEM((total, wide), BF16),
        dma((16,)),
    ]
    sent = call(
        functools.partial(wgrad_kernel, chunks=8, came=False),
        shape((3 * hid, width), BF16),
        "wgrad_away",
        scratch=scratch,
        specs=[any_spec] * 16 + [vmem] * 2,
        cost=(2 * total * width * 3 * hid, 12 * 10**6),
    )(*xs, *ys, away, hidden)
    o_r, f, sent, right = lax.optimization_barrier((o_r, f, sent, right))
    came = hop(sent, C_SWAP)
    oz = hop(join(other, ol, o_r), Z_SWAP)
    lf, r = hop(join(left, f), X_DOWN), hop(right, X_UP)
    last = call(
        functools.partial(last_kernel, group=group),
        shape((LANES, CAP * group + LANES), BF16),
        "last",
        cost=(10**8, 3 * 10**6),
    )(own, r, lf, oz)
    last, mine = lax.optimization_barrier((last, mine))
    back = exchange(last)
    g_grad, u_grad, d_grad = call(
        functools.partial(wgrad_kernel, chunks=8, came=True),
        [shape((hid, width), BF16)] * 3,
        "wgrad_mine",
        scratch=scratch,
        specs=[any_spec] * 16 + [vmem] * 3,
        cost=(2 * total * width * 3 * hid, 15 * 10**6),
    )(*xs, *ys, mine, hidden, came)
    back, g_grad, u_grad, d_grad = lax.optimization_barrier((back, g_grad, u_grad, d_grad))
    token_grad, gate_t = call(
        functools.partial(final_kernel, group=group),
        [shape(tokens.shape, BF16), shape(ids_t.shape, BF16)],
        "final",
        cost=(6 * 10**8, 2 * 10**6),
    )(ids_t, back)
    return (token_grad, gate_t.T, g_grad[None], u_grad[None], d_grad[None])


def solution(mesh):
    tok = P(("edp", "ep"), None)
    wgt = P("ep", "edp", None)
    return jax.shard_map(
        per_device,
        mesh=mesh,
        in_specs=(tok, tok, tok, tok, wgt, wgt, wgt),
        out_specs=(tok, tok, wgt, wgt, wgt),
        check_vma=False,
    )
```

```python
import functools

import jax
import jax.numpy as jnp
from jax import lax
from jax.experimental import pallas as pl
from jax.experimental.pallas import tpu as pltpu
from jax.sharding import PartitionSpec as P

CAP = 3
QN = 8
LANES = 128
F32 = jnp.float32
BF16 = jnp.bfloat16


def chip_perm(move):
    return [(i, (i & 9) | (move((i >> 1) & 3) << 1)) for i in range(16)]


ROW_SWAP = chip_perm(lambda x: 3 - x)
PAIR_SWAP = chip_perm(lambda x: x ^ 1)
Z_SWAP = [(i, i ^ 8) for i in range(16)]
C_SWAP = [(i, i ^ 1) for i in range(16)]


def hop(a, perm):
    return lax.ppermute(a, "edp", perm)


def iota(shape, dim):
    return lax.broadcasted_iota(jnp.int32, shape, dim)


def dot(a, b):
    return jnp.dot(a, b, preferred_element_type=F32)


def dot_nt(a, b):
    return lax.dot_general(a, b, (((1,), (1,)), ((), ())), preferred_element_type=F32)


def call(kernel, outs, name, scratch=(), specs=None, out_specs=None, cost=None, limit=48):
    one = pl.BlockSpec(memory_space=pltpu.VMEM)
    params = pltpu.CompilerParams(vmem_limit_bytes=limit * 1024 * 1024)

    def run(*args):
        return pl.pallas_call(
            kernel,
            out_shape=outs,
            in_specs=[one] * len(args) if specs is None else specs,
            out_specs=jax.tree.map(lambda _: one, outs) if out_specs is None else out_specs,
            scratch_shapes=scratch,
            compiler_params=params,
            name=name,
            cost_estimate=cost
            and pl.CostEstimate(flops=cost[0], bytes_accessed=cost[1], transcendentals=0),
        )(*args)

    return run


def live_tables(ids_t):
    tokens = ids_t.shape[1]
    expert = iota((LANES, tokens), 0) >> 3
    hits = jnp.zeros((LANES, tokens), F32)
    for r in range(ids_t.shape[0]):
        hits = hits + jnp.where(ids_t[r : r + 1, :] == expert, 1.0, 0.0)
    earlier = jnp.where(iota((tokens, tokens), 0) < iota((tokens, tokens), 1), 1.0, 0.0)
    before = dot(hits.astype(BF16), earlier.astype(BF16))
    return [jnp.where(before == s, hits, 0.0) for s in range(CAP)]


def send_kernel(*refs, with_p):
    if with_p:
        ids_ref, probs_ref, tok_ref, out_ref = refs
    else:
        ids_ref, tok_ref, out_ref = refs
    ids_t = ids_ref[...]
    group = tok_ref.shape[1] // QN
    live = live_tables(ids_t)
    q = iota(live[0].shape, 0) & (QN - 1)
    for s in range(CAP):
        total = jnp.zeros((LANES, group), F32)
        for k in range(QN):
            pick = jnp.where(q == k, live[s], 0.0).astype(BF16)
            total = total + dot(pick, tok_ref[:, k * group : (k + 1) * group])
        out_ref[:, s * group : (s + 1) * group] = total.astype(BF16)
    if with_p:
        expert = iota(live[0].shape, 0) >> 3
        probs = jnp.zeros(live[0].shape, F32)
        for r in range(ids_t.shape[0]):
            probs = probs + jnp.where(
                ids_t[r : r + 1, :] == expert, probs_ref[r : r + 1, :].astype(F32), 0.0
            )
        lane = iota((LANES, LANES), 1)
        tail = jnp.zeros((LANES, LANES), F32)
        for s in range(CAP):
            col = jnp.sum(live[s] * probs, axis=1, keepdims=True)
            tail = tail + jnp.where(lane == s, col, 0.0)
        out_ref[:, CAP * group :] = tail.astype(BF16)


def unpack_kernel(in_ref, out_ref, *, group):
    row, col = iota((LANES, LANES), 0), iota((LANES, LANES), 1)
    swap = jnp.where((row & 15) * QN + (row >> 4) == col, 1.0, 0.0).astype(BF16)
    for s in range(CAP):
        got = dot(swap, in_ref[:, s * group : (s + 1) * group]).astype(BF16)
        for k in range(QN):
            out_ref[s * 16 : (s + 1) * 16, k * group : (k + 1) * group] = got[
                k * 16 : (k + 1) * 16, :
            ]
    if out_ref.shape[1] > QN * group:
        tail = dot(swap, in_ref[:, CAP * group :])
        for s in range(CAP):
            out_ref[s * 16 : (s + 1) * 16, QN * group :] = jnp.broadcast_to(
                tail[0:16, s : s + 1], (16, LANES)
            ).astype(BF16)


def fetch(copies):
    for c in copies:
        c.start()
    for c in copies:
        c.wait()


def product(out_ref, left, right, step=640):
    out_ref[...] = jnp.zeros(out_ref.shape, F32)

    def body(n, carry):
        cols = pl.ds(pl.multiple_of(n * step, step), step)
        out_ref[...] += dot_nt(left[:, cols], right[:, cols])
        return carry

    lax.fori_loop(0, left.shape[1] // step, body, 0)


def stacked(sources, target, sems, first):
    rows = sources[0].shape[0]
    return [
        pltpu.make_async_copy(a, target.at[pl.ds(k * rows, rows)], sems.at[first + k])
        for k, a in enumerate(sources)
    ]


def pre_kernel(*refs):
    xs, gs, us = refs[0:4], refs[4:8], refs[8:12]
    gate_ref, up_ref, x_out, g_all, u_all, sems = refs[12:]
    first = stacked(xs, x_out, sems, 0) + stacked(gs, g_all, sems, 4)
    second = stacked(us, u_all, sems, 8)
    for c in first + second:
        c.start()
    for c in first:
        c.wait()
    product(gate_ref, g_all, x_out)
    for c in second:
        c.wait()
    product(up_ref, u_all, x_out)


def main_kernel(*refs):
    ys, ds, (gate_ref, up_ref) = refs[0:4], refs[4:8], refs[8:10]
    dg_ref, du_ref, hid_ref, py_ref, tail_ref, y_all, d_all, acc, sems = refs[10:]
    copies = stacked(ds, d_all, sems, 0) + stacked(ys, y_all, sems, 4)
    fetch(copies)
    width = d_all.shape[1]
    total = y_all.shape[0]
    product(acc, d_all, y_all)
    back = acc[...]
    probs = y_all[:, width:].astype(F32)
    prob = jnp.transpose(probs)[0:1, :]
    gate, up = gate_ref[...], up_ref[...]
    sig = jax.nn.sigmoid(gate)
    hidden = gate * sig * up
    part = jnp.sum(hidden * back, axis=0, keepdims=True)
    scaled = prob * back
    dg_ref[...] = (scaled * up * sig * (1.0 + gate * (1.0 - sig))).astype(BF16)
    du_ref[...] = (scaled * gate * sig).astype(BF16)
    hid_ref[...] = hidden.astype(BF16)
    py_ref[...] = (probs[:, 0:1] * y_all[:, 0:width].astype(F32)).astype(BF16)
    high = part.astype(BF16).astype(F32)
    low = part - high
    tail = jnp.where(
        iota((LANES, total), 0) < LANES // 2,
        jnp.broadcast_to(high, (LANES, total)),
        jnp.broadcast_to(low, (LANES, total)),
    )
    tail_ref[...] = jnp.transpose(tail).astype(BF16)


def back_kernel(*refs):
    dg_ref, du_ref, tail_ref = refs[0:3]
    gs, us, outs = refs[3:7], refs[7:11], refs[11:15]
    g_all, u_all, sems = refs[15:]
    copies = stacked(gs, g_all, sems, 0) + stacked(us, u_all, sems, 4)
    for c in copies:
        c.start()
    rows, width = outs[0].shape[0], g_all.shape[1]
    for k in range(4):
        outs[k][:, width:] = tail_ref[k * rows : (k + 1) * rows, :]
    d_gate = jnp.transpose(dg_ref[...].astype(F32)).astype(BF16)
    d_up = jnp.transpose(du_ref[...].astype(F32)).astype(BF16)
    for c in copies:
        c.wait()
    step = 640

    def body(n, carry):
        cols = pl.ds(pl.multiple_of(n * step, step), step)
        got = (dot(d_gate, g_all[:, cols]) + dot(d_up, u_all[:, cols])).astype(BF16)
        for k in range(4):
            outs[k][:, cols] = got[k * rows : (k + 1) * rows, :]
        return carry

    lax.fori_loop(0, width // step, body, 0)


def wgrad_kernel(left_ref, rows_ref, *rest, first):
    *came, out_ref = rest
    hid = out_ref.shape[0]
    total = dot(left_ref[first : first + hid, :], rows_ref[...])
    for c in came:
        total = total + c[...].astype(F32)
    out_ref[...] = total.astype(BF16)


def summed(refs):
    total = refs[0][...].astype(F32)
    for r in refs[1:]:
        total = total + r[...].astype(F32)
    return total


def join_kernel(*refs, width):
    *parts, out_ref = refs
    body = [p.at[:, pl.ds(0, width)] for p in parts]
    out_ref[:, 0:width] = summed(body).astype(BF16)
    tail = summed([p.at[:, pl.ds(width, LANES)] for p in parts])
    value = tail[:, 0:1] + tail[:, LANES // 2 : LANES // 2 + 1]
    high = value.astype(BF16).astype(F32)
    out_ref[:, width:] = jnp.where(
        iota(tail.shape, 1) < LANES // 2, high, value - high
    ).astype(BF16)


def last_kernel(*refs, group):
    *parts, out_ref = refs
    width = QN * group
    row, col = iota((LANES, LANES), 0), iota((LANES, LANES), 1)
    swap = jnp.where((col & 15) * QN + (col >> 4) == row, 1.0, 0.0).astype(BF16)
    total = summed([p.at[:, pl.ds(0, width)] for p in parts]).astype(BF16)
    for s in range(CAP):
        stack = jnp.concatenate(
            [total[s * 16 : (s + 1) * 16, k * group : (k + 1) * group] for k in range(QN)], axis=0
        )
        out_ref[:, s * group : (s + 1) * group] = dot(swap, stack).astype(BF16)
    tail = summed([p.at[:, pl.ds(width, LANES)] for p in parts])
    value = tail[:, 0:1] + tail[:, LANES // 2 : LANES // 2 + 1]
    lane = iota((16, LANES), 1)
    cols = jnp.zeros((16, LANES), F32)
    for s in range(CAP):
        cols = cols + jnp.where(lane == s, value[s * 16 : (s + 1) * 16, :], 0.0)
    stack = jnp.concatenate([cols] * QN, axis=0).astype(BF16)
    out_ref[:, CAP * group :] = dot(swap, stack).astype(BF16)


def final_kernel(ids_ref, in_ref, tok_ref, gate_ref, *, group):
    ids_t = ids_ref[...]
    live = live_tables(ids_t)
    lane = iota(live[0].shape, 1)
    sides = [jnp.transpose(v) for v in live]
    for k in range(QN):
        total = jnp.zeros((live[0].shape[1], group), F32)
        for s in range(CAP):
            pick = jnp.where((lane & (QN - 1)) == k, sides[s], 0.0).astype(BF16)
            total = total + dot(pick, in_ref[:, s * group : (s + 1) * group])
        tok_ref[:, k * group : (k + 1) * group] = total.astype(BF16)
    row = iota(live[0].shape, 0)
    value = jnp.zeros(live[0].shape, F32)
    for s in range(CAP):
        col = in_ref[:, CAP * group + s : CAP * group + s + 1].astype(F32)
        value = value + live[s] * col
    value = jnp.where((row & (QN - 1)) == 0, value, 0.0)
    for r in range(ids_t.shape[0]):
        mine = jnp.where(ids_t[r : r + 1, :] == (row >> 3), value, 0.0)
        gate_ref[r : r + 1, :] = jnp.sum(mine, axis=0, keepdims=True).astype(BF16)


def per_device(tokens, cotangent, gate_probs, expert_ids, w_gate, w_up, w_down):
    width = tokens.shape[1]
    group = width // QN
    wide = width + LANES
    rows = CAP * 16
    total = 4 * rows
    g, u, d = w_gate[0], w_up[0], w_down[0]
    hid = g.shape[0]
    ids_t, probs_t = expert_ids.T, gate_probs.T
    shape = jax.ShapeDtypeStruct
    any_spec, vmem = pl.BlockSpec(memory_space=pl.ANY), pl.BlockSpec(memory_space=pltpu.VMEM)
    dma = pltpu.SemaphoreType.DMA
    together = lax.optimization_barrier
    work = 2 * total * width * 4 * hid

    def exchange(a):
        a = a.reshape(16, QN, a.shape[1])
        a = lax.all_to_all(a, "ep", split_axis=0, concat_axis=0, tiled=True)
        return a.reshape(LANES, a.shape[2])

    def unpack(a, columns, name):
        return call(
            functools.partial(unpack_kernel, group=group),
            shape((rows, columns), BF16),
            name,
            cost=(10**8, 10**6),
        )(a)

    send_x = call(
        functools.partial(send_kernel, with_p=False),
        shape((LANES, CAP * group), BF16),
        "send_x",
        cost=(6 * 10**8, 2 * 10**6),
    )(ids_t, tokens)
    send_y = call(
        functools.partial(send_kernel, with_p=True),
        shape((LANES, CAP * group + LANES), BF16),
        "send_y",
        cost=(6 * 10**8, 2 * 10**6),
    )(ids_t, probs_t, cotangent)

    core_g, core_u, core_d = hop(g, C_SWAP), hop(u, C_SWAP), hop(d, C_SWAP)
    pair_g = hop(g, PAIR_SWAP)
    got_x, core_g, core_u, core_d, pair_g, send_y, u_next = together(
        (exchange(send_x), core_g, core_u, core_d, pair_g, send_y, u)
    )
    got_y = exchange(send_y)
    x = unpack(got_x, width, "unpack_x")
    x_row, x_oth = hop(x, ROW_SWAP), hop(x, Z_SWAP)
    pair_u = hop(u_next, PAIR_SWAP)
    cross_g = hop(pair_g, C_SWAP)
    got_y, x_row, x_oth, pair_u, cross_g, d_next = together(
        (got_y, x_row, x_oth, pair_u, cross_g, d)
    )
    pair_d = hop(d_next, PAIR_SWAP)
    cross_u = hop(pair_u, C_SWAP)
    y = unpack(got_y, wide, "unpack_y")
    x_oth_row = hop(x_oth, ROW_SWAP)
    y_oth, y_row = hop(y, Z_SWAP), hop(y, ROW_SWAP)
    y_oth_row = hop(y_oth, ROW_SWAP)
    cross_d = hop(pair_d, C_SWAP)
    gs, us = (g, core_g, pair_g, cross_g), (u, core_u, pair_u, cross_u)
    gate, up, x_all = call(
        pre_kernel,
        [shape((4 * hid, total), F32)] * 2 + [shape((total, width), BF16)],
        "pre",
        scratch=[pltpu.VMEM((4 * hid, width), BF16)] * 2 + [dma((12,))],
        specs=[any_spec] * 12,
        cost=(2 * work, 10 * 10**6),
    )(x, x_row, x_oth, x_oth_row, *gs, *us)
    d_gate, d_up, hidden, py, tail = call(
        main_kernel,
        [shape((4 * hid, total), BF16)] * 3
        + [shape((total, width), BF16), shape((total, LANES), BF16)],
        "main",
        scratch=[
            pltpu.VMEM((total, wide), BF16),
            pltpu.VMEM((4 * hid, width), BF16),
            pltpu.VMEM((4 * hid, total), F32),
            dma((8,)),
        ],
        specs=[any_spec] * 8 + [vmem] * 2,
        cost=(work, 8 * 10**6),
    )(y, y_row, y_oth, y_oth_row, d, core_d, pair_d, cross_d, gate, up)

    blocks = 4

    def wgrad(left, right, place, *came):
        cols = width // blocks
        part = pl.BlockSpec((hid, cols), lambda n: (0, n))
        return pl.pallas_call(
            functools.partial(wgrad_kernel, first=place * hid),
            out_shape=shape((hid, width), BF16),
            grid=(blocks,),
            in_specs=[
                pl.BlockSpec(left.shape, lambda n: (0, 0)),
                pl.BlockSpec((total, cols), lambda n: (0, n)),
            ]
            + [part] * len(came),
            out_specs=part,
            compiler_params=pltpu.CompilerParams(vmem_limit_bytes=16 * 1024 * 1024),
            name="wgrad",
            cost_estimate=pl.CostEstimate(
                flops=work // 4, bytes_accessed=3 * 10**6, transcendentals=0
            ),
        )(left, right, *came)

    def join(*a):
        return call(
            functools.partial(join_kernel, width=width),
            shape((rows, wide), BF16),
            "join",
            cost=(10**6, 10**6),
        )(*a)

    cross = [hop(wgrad(hidden, py, 3), C_SWAP)]
    own, row, oth, oth_row = call(
        back_kernel,
        [shape((rows, wide), BF16)] * 4,
        "back",
        scratch=[pltpu.VMEM((4 * hid, width), BF16)] * 2 + [dma((8,))],
        specs=[vmem] * 3 + [any_spec] * 8,
        cost=(2 * work, 10 * 10**6),
    )(d_gate, d_up, tail, *gs, *us)
    cross += [hop(wgrad(d_gate, x_all, 3), C_SWAP), hop(wgrad(d_up, x_all, 3), C_SWAP)]
    far = hop(oth_row, ROW_SWAP)
    pair_dw = hop(wgrad(hidden, py, 2, cross[0]), PAIR_SWAP)
    oth = hop(join(oth, far), Z_SWAP)
    row = hop(row, ROW_SWAP)
    pair_gw = hop(wgrad(d_gate, x_all, 2, cross[1]), PAIR_SWAP)
    pair_uw = hop(wgrad(d_up, x_all, 2, cross[2]), PAIR_SWAP)
    side = [
        hop(wgrad(hidden, py, 1), C_SWAP),
        hop(wgrad(d_gate, x_all, 1), C_SWAP),
        hop(wgrad(d_up, x_all, 1), C_SWAP),
    ]
    last = call(
        functools.partial(last_kernel, group=group),
        shape((LANES, CAP * group + LANES), BF16),
        "last",
        cost=(10**8, 3 * 10**6),
    )(own, row, oth)
    back = exchange(last)
    d_grad = wgrad(hidden, py, 0, side[0], pair_dw)
    g_grad = wgrad(d_gate, x_all, 0, side[1], pair_gw)
    token_grad, gate_t = call(
        functools.partial(final_kernel, group=group),
        [shape(tokens.shape, BF16), shape(ids_t.shape, BF16)],
        "final",
        cost=(6 * 10**8, 2 * 10**6),
    )(ids_t, back)
    u_grad = wgrad(d_up, x_all, 0, side[2], pair_uw)
    return (token_grad, gate_t.T, g_grad[None], u_grad[None], d_grad[None])


def solution(mesh):
    tok = P(("edp", "ep"), None)
    wgt = P("ep", "edp", None)
    return jax.shard_map(
        per_device,
        mesh=mesh,
        in_specs=(tok, tok, tok, tok, wgt, wgt, wgt),
        out_specs=(tok, tok, wgt, wgt, wgt),
        check_vma=False,
    )
```

```python
import functools

import jax
import jax.numpy as jnp
from jax import lax
from jax.experimental import pallas as pl
from jax.experimental.pallas import tpu as pltpu
from jax.sharding import PartitionSpec as P

CAP = 3
QN = 8
LANES = 128
F32 = jnp.float32
BF16 = jnp.bfloat16


def chip_perm(move):
    return [(i, (i & 9) | (move((i >> 1) & 3) << 1)) for i in range(16)]


X_UP = chip_perm(lambda x: (x + 1) % 4)
X_DOWN = chip_perm(lambda x: (x + 3) % 4)
Z_SWAP = [(i, i ^ 8) for i in range(16)]
C_SWAP = [(i, i ^ 1) for i in range(16)]


def hop(a, perm):
    return lax.ppermute(a, "edp", perm)


def iota(shape, dim):
    return lax.broadcasted_iota(jnp.int32, shape, dim)


def dot(a, b):
    return jnp.dot(a, b, preferred_element_type=F32)


def dot_nt(a, b):
    return lax.dot_general(a, b, (((1,), (1,)), ((), ())), preferred_element_type=F32)


def call(kernel, outs, name, scratch=(), specs=None, out_specs=None, cost=None, limit=48):
    one = pl.BlockSpec(memory_space=pltpu.VMEM)
    params = pltpu.CompilerParams(vmem_limit_bytes=limit * 1024 * 1024)

    def run(*args):
        return pl.pallas_call(
            kernel,
            out_shape=outs,
            in_specs=[one] * len(args) if specs is None else specs,
            out_specs=jax.tree.map(lambda _: one, outs) if out_specs is None else out_specs,
            scratch_shapes=scratch,
            compiler_params=params,
            name=name,
            cost_estimate=cost
            and pl.CostEstimate(flops=cost[0], bytes_accessed=cost[1], transcendentals=0),
        )(*args)

    return run


def live_tables(ids_t):
    tokens = ids_t.shape[1]
    expert = iota((LANES, tokens), 0) >> 3
    hits = jnp.zeros((LANES, tokens), F32)
    for r in range(ids_t.shape[0]):
        hits = hits + jnp.where(ids_t[r : r + 1, :] == expert, 1.0, 0.0)
    earlier = jnp.where(iota((tokens, tokens), 0) < iota((tokens, tokens), 1), 1.0, 0.0)
    before = dot(hits.astype(BF16), earlier.astype(BF16))
    return [jnp.where(before == s, hits, 0.0) for s in range(CAP)]


def send_kernel(*refs, with_p):
    if with_p:
        ids_ref, probs_ref, tok_ref, out_ref = refs
    else:
        ids_ref, tok_ref, out_ref = refs
    ids_t = ids_ref[...]
    group = tok_ref.shape[1] // QN
    live = live_tables(ids_t)
    q = iota(live[0].shape, 0) & (QN - 1)
    for s in range(CAP):
        total = jnp.zeros((LANES, group), F32)
        for k in range(QN):
            pick = jnp.where(q == k, live[s], 0.0).astype(BF16)
            total = total + dot(pick, tok_ref[:, k * group : (k + 1) * group])
        out_ref[:, s * group : (s + 1) * group] = total.astype(BF16)
    if with_p:
        expert = iota(live[0].shape, 0) >> 3
        probs = jnp.zeros(live[0].shape, F32)
        for r in range(ids_t.shape[0]):
            probs = probs + jnp.where(
                ids_t[r : r + 1, :] == expert, probs_ref[r : r + 1, :].astype(F32), 0.0
            )
        lane = iota((LANES, LANES), 1)
        tail = jnp.zeros((LANES, LANES), F32)
        for s in range(CAP):
            col = jnp.sum(live[s] * probs, axis=1, keepdims=True)
            tail = tail + jnp.where(lane == s, col, 0.0)
        out_ref[:, CAP * group :] = tail.astype(BF16)


def unpack_kernel(in_ref, out_ref, *, group):
    row, col = iota((LANES, LANES), 0), iota((LANES, LANES), 1)
    swap = jnp.where((row & 15) * QN + (row >> 4) == col, 1.0, 0.0).astype(BF16)
    for s in range(CAP):
        got = dot(swap, in_ref[:, s * group : (s + 1) * group]).astype(BF16)
        for k in range(QN):
            out_ref[s * 16 : (s + 1) * 16, k * group : (k + 1) * group] = got[
                k * 16 : (k + 1) * 16, :
            ]
    if out_ref.shape[1] > QN * group:
        tail = dot(swap, in_ref[:, CAP * group :])
        for s in range(CAP):
            out_ref[s * 16 : (s + 1) * 16, QN * group :] = jnp.broadcast_to(
                tail[0:16, s : s + 1], (16, LANES)
            ).astype(BF16)


BLOCKS = 4


def stacked(sources, target, sems, n):
    rows, width = sources[0].shape
    step = (width // BLOCKS) // LANES * LANES
    start = n * step
    size = step if n < BLOCKS - 1 else width - start
    return [
        pltpu.make_async_copy(
            a.at[:, pl.ds(start, size)],
            target.at[pl.ds(k * rows, rows), pl.ds(start, size)],
            sems.at[k * BLOCKS + n],
        )
        for k, a in enumerate(sources)
    ]


def ready(*copies):
    for group in copies:
        for c in group:
            c.wait()


def pre_kernel(*refs):
    xs, ws = refs[0:8], refs[8:12]
    gate_ref, up_ref, x_out, w_all, x_sems, w_sems = refs[12:]
    x_plan = [stacked(xs, x_out, x_sems, n) for n in range(BLOCKS)]
    w_plan = [stacked(ws, w_all, w_sems, n) for n in range(BLOCKS)]
    for n in range(BLOCKS):
        for c in w_plan[n] + x_plan[n]:
            c.start()
    step = x_out.shape[1] // BLOCKS
    half = w_all.shape[0] // 2
    for n in range(BLOCKS):
        ready(w_plan[n], x_plan[n])
        cols = slice(n * step, (n + 1) * step)
        for out_ref, first in ((gate_ref, 0), (up_ref, half)):
            got = dot_nt(w_all[first : first + half, cols], x_out[:, cols])
            if n == 0:
                out_ref[...] = got
            else:
                out_ref[...] += got


def main_kernel(*refs):
    ys, ds, ws, (gate_ref, up_ref) = refs[0:8], refs[8:10], refs[10:14], refs[14:16]
    outs, (dg_ref, du_ref, hid_ref, py_ref) = refs[16:24], refs[24:28]
    y_all, d_all, w_all, acc, y_sems, d_sems, w_sems = refs[28:]
    y_plan = [stacked(ys, y_all, y_sems, n) for n in range(BLOCKS)]
    d_plan = [stacked(ds, d_all, d_sems, n) for n in range(BLOCKS)]
    w_plan = [stacked(ws, w_all, w_sems, n) for n in range(BLOCKS)]
    for n in range(BLOCKS):
        for c in d_plan[n] + y_plan[n]:
            c.start()
    for n in range(BLOCKS):
        for c in w_plan[n]:
            c.start()
    width, total = d_all.shape[1], y_all.shape[0]
    rows = total // 8
    step = width // BLOCKS
    for n in range(BLOCKS):
        ready(d_plan[n], y_plan[n])
        cols = slice(n * step, (n + 1) * step)
        got = dot_nt(d_all[:, cols], y_all[:, cols])
        if n == 0:
            acc[...] = got
        else:
            acc[...] += got
    back = acc[...]
    probs = y_all[:, width:].astype(F32)
    prob = jnp.transpose(probs)[0:1, :]
    gate, up = gate_ref[...], up_ref[...]
    sig = jax.nn.sigmoid(gate)
    hidden = gate * sig * up
    part = jnp.sum(hidden * back, axis=0, keepdims=True)
    scaled = prob * back
    d_gate = scaled * up * sig * (1.0 + gate * (1.0 - sig))
    d_up = scaled * gate * sig
    hid_ref[...] = hidden.astype(BF16)
    dg_ref[...] = d_gate.astype(BF16)
    du_ref[...] = d_up.astype(BF16)
    both = jnp.transpose(jnp.concatenate([d_gate, d_up], axis=0)).astype(BF16)
    high = part.astype(BF16).astype(F32)
    tail = jnp.where(
        iota((LANES, total), 0) < LANES // 2,
        jnp.broadcast_to(high, (LANES, total)),
        jnp.broadcast_to(part - high, (LANES, total)),
    )
    tail = jnp.transpose(tail).astype(BF16)
    for k in range(8):
        outs[k][:, width:] = tail[k * rows : (k + 1) * rows, :]
    prob_col = probs[:, 0:1]
    for n in range(BLOCKS):
        ready(w_plan[n])
        for m in range(2):
            cols = slice(n * step + m * step // 2, n * step + (m + 1) * step // 2)
            got = dot(both, w_all[:, cols]).astype(BF16)
            for k in range(8):
                outs[k][:, cols] = got[k * rows : (k + 1) * rows, :]
            py_ref[:, cols] = (prob_col * y_all[:, cols].astype(F32)).astype(BF16)


def wgrad_kernel(left_ref, rows_ref, *rest, first):
    *came, out_ref = rest
    hid = out_ref.shape[0]
    total = dot(left_ref[first : first + hid, :], rows_ref[...])
    for c in came:
        total = total + c[...].astype(F32)
    out_ref[...] = total.astype(BF16)


def summed(refs):
    total = refs[0][...].astype(F32)
    for r in refs[1:]:
        total = total + r[...].astype(F32)
    return total


def join_kernel(*refs, width):
    *parts, out_ref = refs
    body = [p.at[:, pl.ds(0, width)] for p in parts]
    out_ref[:, 0:width] = summed(body).astype(BF16)
    tail = summed([p.at[:, pl.ds(width, LANES)] for p in parts])
    value = tail[:, 0:1] + tail[:, LANES // 2 : LANES // 2 + 1]
    high = value.astype(BF16).astype(F32)
    out_ref[:, width:] = jnp.where(
        iota(tail.shape, 1) < LANES // 2, high, value - high
    ).astype(BF16)


def last_kernel(*refs, group):
    *parts, out_ref = refs
    width = QN * group
    row, col = iota((LANES, LANES), 0), iota((LANES, LANES), 1)
    swap = jnp.where((col & 15) * QN + (col >> 4) == row, 1.0, 0.0).astype(BF16)
    total = summed([p.at[:, pl.ds(0, width)] for p in parts]).astype(BF16)
    for s in range(CAP):
        stack = jnp.concatenate(
            [total[s * 16 : (s + 1) * 16, k * group : (k + 1) * group] for k in range(QN)], axis=0
        )
        out_ref[:, s * group : (s + 1) * group] = dot(swap, stack).astype(BF16)
    tail = summed([p.at[:, pl.ds(width, LANES)] for p in parts])
    value = tail[:, 0:1] + tail[:, LANES // 2 : LANES // 2 + 1]
    lane = iota((16, LANES), 1)
    cols = jnp.zeros((16, LANES), F32)
    for s in range(CAP):
        cols = cols + jnp.where(lane == s, value[s * 16 : (s + 1) * 16, :], 0.0)
    stack = jnp.concatenate([cols] * QN, axis=0).astype(BF16)
    out_ref[:, CAP * group :] = dot(swap, stack).astype(BF16)


def final_kernel(ids_ref, in_ref, tok_ref, gate_ref, *, group):
    ids_t = ids_ref[...]
    live = live_tables(ids_t)
    lane = iota(live[0].shape, 1)
    sides = [jnp.transpose(v) for v in live]
    for k in range(QN):
        total = jnp.zeros((live[0].shape[1], group), F32)
        for s in range(CAP):
            pick = jnp.where((lane & (QN - 1)) == k, sides[s], 0.0).astype(BF16)
            total = total + dot(pick, in_ref[:, s * group : (s + 1) * group])
        tok_ref[:, k * group : (k + 1) * group] = total.astype(BF16)
    row = iota(live[0].shape, 0)
    value = jnp.zeros(live[0].shape, F32)
    for s in range(CAP):
        col = in_ref[:, CAP * group + s : CAP * group + s + 1].astype(F32)
        value = value + live[s] * col
    value = jnp.where((row & (QN - 1)) == 0, value, 0.0)
    for r in range(ids_t.shape[0]):
        mine = jnp.where(ids_t[r : r + 1, :] == (row >> 3), value, 0.0)
        gate_ref[r : r + 1, :] = jnp.sum(mine, axis=0, keepdims=True).astype(BF16)


def per_device(tokens, cotangent, gate_probs, expert_ids, w_gate, w_up, w_down):
    width = tokens.shape[1]
    group = width // QN
    wide = width + LANES
    rows = CAP * 16
    total = 8 * rows
    g, u, d = w_gate[0], w_up[0], w_down[0]
    hid = g.shape[0]
    ids_t, probs_t = expert_ids.T, gate_probs.T
    shape = jax.ShapeDtypeStruct
    any_spec, vmem = pl.BlockSpec(memory_space=pl.ANY), pl.BlockSpec(memory_space=pltpu.VMEM)
    dma = pltpu.SemaphoreType.DMA
    together = lax.optimization_barrier
    work = 2 * total * width * 2 * hid

    def exchange(a):
        a = a.reshape(16, QN, a.shape[1])
        a = lax.all_to_all(a, "ep", split_axis=0, concat_axis=0, tiled=True)
        return a.reshape(LANES, a.shape[2])

    def unpack(a, columns, name):
        return call(
            functools.partial(unpack_kernel, group=group),
            shape((rows, columns), BF16),
            name,
            cost=(10**8, 10**6),
        )(a)

    send_x = call(
        functools.partial(send_kernel, with_p=False),
        shape((LANES, CAP * group), BF16),
        "send_x",
        cost=(6 * 10**8, 2 * 10**6),
    )(ids_t, tokens)
    core_g, core_u, core_d = hop(g, C_SWAP), hop(u, C_SWAP), hop(d, C_SWAP)
    got_x, core_g, core_u, core_d = together((exchange(send_x), core_g, core_u, core_d))
    x = unpack(got_x, width, "unpack_x")
    left, right, oth = hop(x, X_UP), hop(x, X_DOWN), hop(x, Z_SWAP)
    x_now, cot_now = together((x, cotangent))
    send_y = call(
        functools.partial(send_kernel, with_p=True),
        shape((LANES, CAP * group + LANES), BF16),
        "send_y",
        cost=(6 * 10**8, 2 * 10**6),
    )(ids_t, probs_t, cot_now)
    got_y = exchange(send_y)
    left, right, oth = together((left, right, oth))
    far, o_right, o_left = hop(left, X_UP), hop(oth, X_DOWN), hop(oth, X_UP)
    far, o_right, got_y = together((far, o_right, got_y))
    o_far = hop(o_right, X_DOWN)
    y = unpack(got_y, wide, "unpack_y")
    y_left, y_right, y_oth = hop(y, X_UP), hop(y, X_DOWN), hop(y, Z_SWAP)
    gate, up, x_all = call(
        pre_kernel,
        [shape((2 * hid, total), F32)] * 2 + [shape((total, width), BF16)],
        "pre",
        scratch=[pltpu.VMEM((4 * hid, width), BF16), dma((32,)), dma((16,))],
        specs=[any_spec] * 12,
        cost=(2 * work, 10 * 10**6),
    )(x, left, far, right, oth, o_left, o_far, o_right, g, core_g, u, core_u)
    y_left, y_right, y_oth, gate = together((y_left, y_right, y_oth, gate))
    y_far, yo_right, yo_left = hop(y_left, X_UP), hop(y_oth, X_DOWN), hop(y_oth, X_UP)
    yo_far = hop(yo_right, X_DOWN)
    *parts, d_gate, d_up, hidden, py = call(
        main_kernel,
        [shape((rows, wide), BF16)] * 8
        + [shape((2 * hid, total), BF16)] * 3
        + [shape((total, width), BF16)],
        "main",
        scratch=[
            pltpu.VMEM((total, wide), BF16),
            pltpu.VMEM((2 * hid, width), BF16),
            pltpu.VMEM((4 * hid, width), BF16),
            pltpu.VMEM((2 * hid, total), F32),
            dma((32,)),
            dma((8,)),
            dma((16,)),
        ],
        specs=[any_spec] * 14 + [vmem] * 2,
        cost=(3 * work, 14 * 10**6),
    )(
        *(y, y_left, y_far, y_right, y_oth, yo_left, yo_far, yo_right),
        *(d, core_d, g, core_g, u, core_u, gate, up),
    )

    blocks = 4

    def wgrad(left, right, place, *came):
        cols = width // blocks
        part = pl.BlockSpec((hid, cols), lambda n: (0, n))
        return pl.pallas_call(
            functools.partial(wgrad_kernel, first=place * hid),
            out_shape=shape((hid, width), BF16),
            grid=(blocks,),
            in_specs=[
                pl.BlockSpec(left.shape, lambda n: (0, 0)),
                pl.BlockSpec((total, cols), lambda n: (0, n)),
            ]
            + [part] * len(came),
            out_specs=part,
            compiler_params=pltpu.CompilerParams(vmem_limit_bytes=16 * 1024 * 1024),
            name="wgrad",
            cost_estimate=pl.CostEstimate(
                flops=work // 4, bytes_accessed=3 * 10**6, transcendentals=0
            ),
        )(left, right, *came)

    def join(*a):
        return call(
            functools.partial(join_kernel, width=width),
            shape((rows, wide), BF16),
            "join",
            cost=(10**6, 10**6),
        )(*a)

    own, left, far, right, oth, o_left, o_far, o_right = parts
    of, ol = hop(o_far, X_UP), hop(o_left, X_DOWN)
    away = [wgrad(hidden, py, 1), wgrad(d_gate, x_all, 1), wgrad(d_up, x_all, 1)]
    of, ol, far, *away = together((of, ol, far, *away))
    o_r, f = hop(join(o_right, of), X_UP), hop(far, X_DOWN)
    came = [hop(a, C_SWAP) for a in away]
    o_r, f, right, hidden, d_gate, d_up, *came = together(
        (o_r, f, right, hidden, d_gate, d_up, *came)
    )
    oz = hop(join(oth, ol, o_r), Z_SWAP)
    lf, r = hop(join(left, f), X_DOWN), hop(right, X_UP)
    d_grad = wgrad(hidden, py, 0, came[0])
    g_grad = wgrad(d_gate, x_all, 0, came[1])
    u_grad = wgrad(d_up, x_all, 0, came[2])
    oz, lf, r, d_grad, g_grad, u_grad = together((oz, lf, r, d_grad, g_grad, u_grad))
    last = call(
        functools.partial(last_kernel, group=group),
        shape((LANES, CAP * group + LANES), BF16),
        "last",
        cost=(10**8, 3 * 10**6),
    )(own, r, lf, oz)
    back = exchange(last)
    token_grad, gate_t = call(
        functools.partial(final_kernel, group=group),
        [shape(tokens.shape, BF16), shape(ids_t.shape, BF16)],
        "final",
        cost=(6 * 10**8, 2 * 10**6),
    )(ids_t, back)
    return (token_grad, gate_t.T, g_grad[None], u_grad[None], d_grad[None])


def solution(mesh):
    tok = P(("edp", "ep"), None)
    wgt = P("ep", "edp", None)
    return jax.shard_map(
        per_device,
        mesh=mesh,
        in_specs=(tok, tok, tok, tok, wgt, wgt, wgt),
        out_specs=(tok, tok, wgt, wgt, wgt),
        check_vma=False,
    )
```

```python
import functools

import jax
import jax.numpy as jnp
from jax import lax
from jax.experimental import pallas as pl
from jax.experimental.pallas import tpu as pltpu
from jax.sharding import PartitionSpec as P

CAP = 3
QN = 8
LANES = 128
F32 = jnp.float32
BF16 = jnp.bfloat16


def x_perm(step):
    pairs = []
    for i in range(16):
        x = ((i >> 1) + (step if i % 2 == 0 else -step)) & 3
        pairs.append((i, (i & 9) | (x << 1)))
    return pairs


X_A, X_B = x_perm(1), x_perm(-1)
Z_SWAP = [(i, i ^ 8) for i in range(16)]
C_SWAP = [(i, i ^ 1) for i in range(16)]


def hop(a, perm):
    return lax.ppermute(a, "edp", perm)


def iota(shape, dim):
    return lax.broadcasted_iota(jnp.int32, shape, dim)


def dot(a, b):
    return jnp.dot(a, b, preferred_element_type=F32)


def dot_nt(a, b):
    return lax.dot_general(a, b, (((1,), (1,)), ((), ())), preferred_element_type=F32)


def call(kernel, outs, name, scratch=(), specs=None, out_specs=None, cost=None, limit=48):
    one = pl.BlockSpec(memory_space=pltpu.VMEM)
    params = pltpu.CompilerParams(vmem_limit_bytes=limit * 1024 * 1024)

    def run(*args):
        return pl.pallas_call(
            kernel,
            out_shape=outs,
            in_specs=[one] * len(args) if specs is None else specs,
            out_specs=jax.tree.map(lambda _: one, outs) if out_specs is None else out_specs,
            scratch_shapes=scratch,
            compiler_params=params,
            name=name,
            cost_estimate=cost
            and pl.CostEstimate(flops=cost[0], bytes_accessed=cost[1], transcendentals=0),
        )(*args)

    return run


def live_tables(ids_t):
    tokens = ids_t.shape[1]
    expert = iota((LANES, tokens), 0) >> 3
    hits = jnp.zeros((LANES, tokens), F32)
    for r in range(ids_t.shape[0]):
        hits = hits + jnp.where(ids_t[r : r + 1, :] == expert, 1.0, 0.0)
    earlier = jnp.where(iota((tokens, tokens), 0) < iota((tokens, tokens), 1), 1.0, 0.0)
    before = dot(hits.astype(BF16), earlier.astype(BF16))
    return [jnp.where(before == s, hits, 0.0) for s in range(CAP)]


def send_kernel(*refs, with_p):
    if with_p:
        ids_ref, probs_ref, tok_ref, out_ref = refs
    else:
        ids_ref, tok_ref, out_ref = refs
    ids_t = ids_ref[...]
    group = tok_ref.shape[1] // QN
    live = live_tables(ids_t)
    q = iota(live[0].shape, 0) & (QN - 1)
    for s in range(CAP):
        total = jnp.zeros((LANES, group), F32)
        for k in range(QN):
            pick = jnp.where(q == k, live[s], 0.0).astype(BF16)
            total = total + dot(pick, tok_ref[:, k * group : (k + 1) * group])
        out_ref[:, s * group : (s + 1) * group] = total.astype(BF16)
    if with_p:
        expert = iota(live[0].shape, 0) >> 3
        probs = jnp.zeros(live[0].shape, F32)
        for r in range(ids_t.shape[0]):
            probs = probs + jnp.where(
                ids_t[r : r + 1, :] == expert, probs_ref[r : r + 1, :].astype(F32), 0.0
            )
        lane = iota((LANES, LANES), 1)
        tail = jnp.zeros((LANES, LANES), F32)
        for s in range(CAP):
            col = jnp.sum(live[s] * probs, axis=1, keepdims=True)
            tail = tail + jnp.where(lane == s, col, 0.0)
        out_ref[:, CAP * group :] = tail.astype(BF16)


def unpack_kernel(in_ref, out_ref, *, group):
    row, col = iota((LANES, LANES), 0), iota((LANES, LANES), 1)
    swap = jnp.where((row & 15) * QN + (row >> 4) == col, 1.0, 0.0).astype(BF16)
    for s in range(CAP):
        got = dot(swap, in_ref[:, s * group : (s + 1) * group]).astype(BF16)
        for k in range(QN):
            out_ref[s * 16 : (s + 1) * 16, k * group : (k + 1) * group] = got[
                k * 16 : (k + 1) * 16, :
            ]
    if out_ref.shape[1] > QN * group:
        tail = dot(swap, in_ref[:, CAP * group :])
        for s in range(CAP):
            out_ref[s * 16 : (s + 1) * 16, QN * group :] = jnp.broadcast_to(
                tail[0:16, s : s + 1], (16, LANES)
            ).astype(BF16)


BLOCKS = 4


def stacked(sources, target, sems, n):
    rows, width = sources[0].shape
    step = (width // BLOCKS) // LANES * LANES
    start = n * step
    size = step if n < BLOCKS - 1 else width - start
    return [
        pltpu.make_async_copy(
            a.at[:, pl.ds(start, size)],
            target.at[pl.ds(k * rows, rows), pl.ds(start, size)],
            sems.at[k * BLOCKS + n],
        )
        for k, a in enumerate(sources)
    ]


def ready(*copies):
    for group in copies:
        for c in group:
            c.wait()


def pre_kernel(*refs):
    xs, ws = refs[0:8], refs[8:12]
    gate_ref, up_ref, x_out, w_all, x_sems, w_sems = refs[12:]
    x_plan = [stacked(xs, x_out, x_sems, n) for n in range(BLOCKS)]
    w_plan = [stacked(ws, w_all, w_sems, n) for n in range(BLOCKS)]
    for n in range(BLOCKS):
        for c in w_plan[n] + x_plan[n]:
            c.start()
    step = x_out.shape[1] // BLOCKS
    half = w_all.shape[0] // 2
    for n in range(BLOCKS):
        ready(w_plan[n], x_plan[n])
        cols = slice(n * step, (n + 1) * step)
        for out_ref, first in ((gate_ref, 0), (up_ref, half)):
            got = dot_nt(w_all[first : first + half, cols], x_out[:, cols])
            if n == 0:
                out_ref[...] = got
            else:
                out_ref[...] += got


def main_kernel(*refs):
    ys, ds, ws, (gate_ref, up_ref) = refs[0:8], refs[8:10], refs[10:14], refs[14:16]
    outs, (dg_ref, du_ref, hid_ref, py_ref) = refs[16:24], refs[24:28]
    y_all, d_all, w_all, acc, y_sems, d_sems, w_sems = refs[28:]
    y_plan = [stacked(ys, y_all, y_sems, n) for n in range(BLOCKS)]
    d_plan = [stacked(ds, d_all, d_sems, n) for n in range(BLOCKS)]
    w_plan = [stacked(ws, w_all, w_sems, n) for n in range(BLOCKS)]
    for n in range(BLOCKS):
        for c in d_plan[n] + y_plan[n]:
            c.start()
    for n in range(BLOCKS):
        for c in w_plan[n]:
            c.start()
    width, total = d_all.shape[1], y_all.shape[0]
    rows = total // 8
    step = width // BLOCKS
    for n in range(BLOCKS):
        ready(d_plan[n], y_plan[n])
        cols = slice(n * step, (n + 1) * step)
        got = dot_nt(d_all[:, cols], y_all[:, cols])
        if n == 0:
            acc[...] = got
        else:
            acc[...] += got
    back = acc[...]
    probs = y_all[:, width:].astype(F32)
    prob = jnp.transpose(probs)[0:1, :]
    gate, up = gate_ref[...], up_ref[...]
    sig = jax.nn.sigmoid(gate)
    hidden = gate * sig * up
    part = jnp.sum(hidden * back, axis=0, keepdims=True)
    scaled = prob * back
    d_gate = scaled * up * sig * (1.0 + gate * (1.0 - sig))
    d_up = scaled * gate * sig
    hid_ref[...] = hidden.astype(BF16)
    dg_ref[...] = d_gate.astype(BF16)
    du_ref[...] = d_up.astype(BF16)
    both = jnp.transpose(jnp.concatenate([d_gate, d_up], axis=0)).astype(BF16)
    high = part.astype(BF16).astype(F32)
    tail = jnp.where(
        iota((LANES, total), 0) < LANES // 2,
        jnp.broadcast_to(high, (LANES, total)),
        jnp.broadcast_to(part - high, (LANES, total)),
    )
    tail = jnp.transpose(tail).astype(BF16)
    for k in range(8):
        outs[k][:, width:] = tail[k * rows : (k + 1) * rows, :]
    prob_col = probs[:, 0:1]
    for n in range(BLOCKS):
        ready(w_plan[n])
        for m in range(2):
            cols = slice(n * step + m * step // 2, n * step + (m + 1) * step // 2)
            got = dot(both, w_all[:, cols]).astype(BF16)
            for k in range(8):
                outs[k][:, cols] = got[k * rows : (k + 1) * rows, :]
            py_ref[:, cols] = (prob_col * y_all[:, cols].astype(F32)).astype(BF16)


def wgrad_kernel(hid_ref, dg_ref, du_ref, py_ref, x_ref, *rest, away):
    hid = hid_ref.shape[0] // 2
    first = hid if away else 0
    sides = ((dg_ref, x_ref), (du_ref, x_ref), (hid_ref, py_ref))
    for i, (left, right) in enumerate(sides):
        total = dot(left[first : first + hid, :], right[...])
        if away:
            rest[0][i * hid : (i + 1) * hid, :] = total.astype(BF16)
        else:
            came = rest[0][i * hid : (i + 1) * hid, :].astype(F32)
            rest[1 + i][...] = (total + came).astype(BF16)


def summed(refs):
    total = refs[0][...].astype(F32)
    for r in refs[1:]:
        total = total + r[...].astype(F32)
    return total


def join_kernel(*refs, width):
    *parts, out_ref = refs
    body = [p.at[:, pl.ds(0, width)] for p in parts]
    out_ref[:, 0:width] = summed(body).astype(BF16)
    tail = summed([p.at[:, pl.ds(width, LANES)] for p in parts])
    value = tail[:, 0:1] + tail[:, LANES // 2 : LANES // 2 + 1]
    high = value.astype(BF16).astype(F32)
    out_ref[:, width:] = jnp.where(
        iota(tail.shape, 1) < LANES // 2, high, value - high
    ).astype(BF16)


def last_kernel(*refs, group):
    *parts, out_ref = refs
    width = QN * group
    row, col = iota((LANES, LANES), 0), iota((LANES, LANES), 1)
    swap = jnp.where((col & 15) * QN + (col >> 4) == row, 1.0, 0.0).astype(BF16)
    total = summed([p.at[:, pl.ds(0, width)] for p in parts]).astype(BF16)
    for s in range(CAP):
        stack = jnp.concatenate(
            [total[s * 16 : (s + 1) * 16, k * group : (k + 1) * group] for k in range(QN)], axis=0
        )
        out_ref[:, s * group : (s + 1) * group] = dot(swap, stack).astype(BF16)
    tail = summed([p.at[:, pl.ds(width, LANES)] for p in parts])
    value = tail[:, 0:1] + tail[:, LANES // 2 : LANES // 2 + 1]
    lane = iota((16, LANES), 1)
    cols = jnp.zeros((16, LANES), F32)
    for s in range(CAP):
        cols = cols + jnp.where(lane == s, value[s * 16 : (s + 1) * 16, :], 0.0)
    stack = jnp.concatenate([cols] * QN, axis=0).astype(BF16)
    out_ref[:, CAP * group :] = dot(swap, stack).astype(BF16)


def final_kernel(ids_ref, in_ref, tok_ref, gate_ref, *, group):
    ids_t = ids_ref[...]
    live = live_tables(ids_t)
    lane = iota(live[0].shape, 1)
    sides = [jnp.transpose(v) for v in live]
    for k in range(QN):
        total = jnp.zeros((live[0].shape[1], group), F32)
        for s in range(CAP):
            pick = jnp.where((lane & (QN - 1)) == k, sides[s], 0.0).astype(BF16)
            total = total + dot(pick, in_ref[:, s * group : (s + 1) * group])
        tok_ref[:, k * group : (k + 1) * group] = total.astype(BF16)
    row = iota(live[0].shape, 0)
    value = jnp.zeros(live[0].shape, F32)
    for s in range(CAP):
        col = in_ref[:, CAP * group + s : CAP * group + s + 1].astype(F32)
        value = value + live[s] * col
    value = jnp.where((row & (QN - 1)) == 0, value, 0.0)
    for r in range(ids_t.shape[0]):
        mine = jnp.where(ids_t[r : r + 1, :] == (row >> 3), value, 0.0)
        gate_ref[r : r + 1, :] = jnp.sum(mine, axis=0, keepdims=True).astype(BF16)


def per_device(tokens, cotangent, gate_probs, expert_ids, w_gate, w_up, w_down):
    width = tokens.shape[1]
    group = width // QN
    wide = width + LANES
    rows = CAP * 16
    total = 8 * rows
    g, u, d = w_gate[0], w_up[0], w_down[0]
    hid = g.shape[0]
    ids_t, probs_t = expert_ids.T, gate_probs.T
    shape = jax.ShapeDtypeStruct
    any_spec, vmem = pl.BlockSpec(memory_space=pl.ANY), pl.BlockSpec(memory_space=pltpu.VMEM)
    dma = pltpu.SemaphoreType.DMA
    together = lax.optimization_barrier
    work = 2 * total * width * 2 * hid

    def exchange(a):
        a = a.reshape(16, QN, a.shape[1])
        a = lax.all_to_all(a, "ep", split_axis=0, concat_axis=0, tiled=True)
        return a.reshape(LANES, a.shape[2])

    def unpack(a, columns, name):
        return call(
            functools.partial(unpack_kernel, group=group),
            shape((rows, columns), BF16),
            name,
            cost=(10**8, 10**6),
        )(a)

    send_x = call(
        functools.partial(send_kernel, with_p=False),
        shape((LANES, CAP * group), BF16),
        "send_x",
        cost=(6 * 10**8, 2 * 10**6),
    )(ids_t, tokens)
    core_g, core_u, core_d = hop(g, C_SWAP), hop(u, C_SWAP), hop(d, C_SWAP)
    got_x, core_g, core_u, core_d = together((exchange(send_x), core_g, core_u, core_d))
    x = unpack(got_x, width, "unpack_x")
    xa, xb, oth = hop(x, X_A), hop(x, X_B), hop(x, Z_SWAP)
    x_now, cot_now = together((x, cotangent))
    send_y = call(
        functools.partial(send_kernel, with_p=True),
        shape((LANES, CAP * group + LANES), BF16),
        "send_y",
        cost=(6 * 10**8, 2 * 10**6),
    )(ids_t, probs_t, cot_now)
    got_y = exchange(send_y)
    xa, xb, oth = together((xa, xb, oth))
    far, oa, ob = hop(xa, X_A), hop(oth, X_A), hop(oth, X_B)
    far, oa, ob, got_y = together((far, oa, ob, got_y))
    y = unpack(got_y, wide, "unpack_y")
    ya, yb, y_oth = hop(y, X_A), hop(y, X_B), hop(y, Z_SWAP)
    ya, yb, y_oth, far = together((ya, yb, y_oth, far))
    y_far, yoa, yob = hop(ya, X_A), hop(y_oth, X_A), hop(y_oth, X_B)
    o_far = hop(far, Z_SWAP)
    y_far, o_far = together((y_far, o_far))
    yo_far = hop(y_far, Z_SWAP)
    gate, up, x_all = call(
        pre_kernel,
        [shape((2 * hid, total), F32)] * 2 + [shape((total, width), BF16)],
        "pre",
        scratch=[pltpu.VMEM((4 * hid, width), BF16), dma((32,)), dma((16,))],
        specs=[any_spec] * 12,
        cost=(2 * work, 10 * 10**6),
    )(x, xa, far, xb, oth, oa, o_far, ob, g, core_g, u, core_u)
    *parts, d_gate, d_up, hidden, py = call(
        main_kernel,
        [shape((rows, wide), BF16)] * 8
        + [shape((2 * hid, total), BF16)] * 3
        + [shape((total, width), BF16)],
        "main",
        scratch=[
            pltpu.VMEM((total, wide), BF16),
            pltpu.VMEM((2 * hid, width), BF16),
            pltpu.VMEM((4 * hid, width), BF16),
            pltpu.VMEM((2 * hid, total), F32),
            dma((32,)),
            dma((8,)),
            dma((16,)),
        ],
        specs=[any_spec] * 14 + [vmem] * 2,
        cost=(3 * work, 14 * 10**6),
    )(
        *(y, ya, y_far, yb, y_oth, yoa, yo_far, yob),
        *(d, core_d, g, core_g, u, core_u, gate, up),
    )

    blocks = 4

    def wgrad(*came):
        cols = width // blocks

        def part(height):
            return pl.BlockSpec((height, cols), lambda n: (0, n))

        left = pl.BlockSpec((2 * hid, total), lambda n: (0, 0))
        out = [shape((hid, width), BF16)] * 3 if came else shape((3 * hid, width), BF16)
        return pl.pallas_call(
            functools.partial(wgrad_kernel, away=not came),
            out_shape=out,
            grid=(blocks,),
            in_specs=[left] * 3 + [part(total)] * 2 + [part(3 * hid)] * len(came),
            out_specs=[part(hid)] * 3 if came else part(3 * hid),
            compiler_params=pltpu.CompilerParams(vmem_limit_bytes=32 * 1024 * 1024),
            name="wgrad_mine" if came else "wgrad_away",
            cost_estimate=pl.CostEstimate(
                flops=work * 3 // 2, bytes_accessed=12 * 10**6, transcendentals=0
            ),
        )(hidden, d_gate, d_up, py, x_all, *came)

    def join(*a):
        return call(
            functools.partial(join_kernel, width=width),
            shape((rows, wide), BF16),
            "join",
            cost=(10**6, 10**6),
        )(*a)

    own, pa, far, pb, oth, oa, o_far, ob = parts
    of, oa, ob = hop(o_far, Z_SWAP), hop(oa, X_B), hop(ob, X_A)
    away = wgrad()
    of, oa, ob, pb, away = together((of, oa, ob, pb, away))
    f, oz = hop(join(far, of), X_B), hop(join(oth, oa, ob), Z_SWAP)
    pb = hop(pb, X_A)
    came = hop(away, C_SWAP)
    f, oz, pb = together((f, oz, pb))
    pa = hop(join(pa, f), X_B)
    last = call(
        functools.partial(last_kernel, group=group),
        shape((LANES, CAP * group + LANES), BF16),
        "last",
        cost=(10**8, 3 * 10**6),
    )(own, pa, pb, oz)
    last, came = together((last, came))
    back = exchange(last)
    g_grad, u_grad, d_grad = wgrad(came)
    back, g_grad, u_grad, d_grad = together((back, g_grad, u_grad, d_grad))
    token_grad, gate_t = call(
        functools.partial(final_kernel, group=group),
        [shape(tokens.shape, BF16), shape(ids_t.shape, BF16)],
        "final",
        cost=(6 * 10**8, 2 * 10**6),
    )(ids_t, back)
    return (token_grad, gate_t.T, g_grad[None], u_grad[None], d_grad[None])


def solution(mesh):
    tok = P(("edp", "ep"), None)
    wgt = P("ep", "edp", None)
    return jax.shard_map(
        per_device,
        mesh=mesh,
        in_specs=(tok, tok, tok, tok, wgt, wgt, wgt),
        out_specs=(tok, tok, wgt, wgt, wgt),
        check_vma=False,
    )
```

```python
import functools

import jax
import jax.numpy as jnp
from jax import lax
from jax.experimental import pallas as pl
from jax.experimental.pallas import tpu as pltpu
from jax.sharding import PartitionSpec as P

CAP = 3
QN = 8
LANES = 128
F32 = jnp.float32
BF16 = jnp.bfloat16


def x_perm(step):
    pairs = []
    for i in range(16):
        x = ((i >> 1) + (step if i % 2 == 0 else -step)) & 3
        pairs.append((i, (i & 9) | (x << 1)))
    return pairs


X_A, X_B = x_perm(1), x_perm(-1)
Z_SWAP = [(i, i ^ 8) for i in range(16)]
C_SWAP = [(i, i ^ 1) for i in range(16)]


def hop(a, perm):
    return lax.ppermute(a, "edp", perm)


def iota(shape, dim):
    return lax.broadcasted_iota(jnp.int32, shape, dim)


def dot(a, b):
    return jnp.dot(a, b, preferred_element_type=F32)


def dot_nt(a, b):
    return lax.dot_general(a, b, (((1,), (1,)), ((), ())), preferred_element_type=F32)


def call(kernel, outs, name, scratch=(), specs=None, out_specs=None, cost=None, limit=48):
    one = pl.BlockSpec(memory_space=pltpu.VMEM)
    params = pltpu.CompilerParams(vmem_limit_bytes=limit * 1024 * 1024)

    def run(*args):
        return pl.pallas_call(
            kernel,
            out_shape=outs,
            in_specs=[one] * len(args) if specs is None else specs,
            out_specs=jax.tree.map(lambda _: one, outs) if out_specs is None else out_specs,
            scratch_shapes=scratch,
            compiler_params=params,
            name=name,
            cost_estimate=cost
            and pl.CostEstimate(flops=cost[0], bytes_accessed=cost[1], transcendentals=0),
        )(*args)

    return run


def live_tables(ids_t):
    tokens = ids_t.shape[1]
    expert = iota((LANES, tokens), 0) >> 3
    hits = jnp.zeros((LANES, tokens), F32)
    for r in range(ids_t.shape[0]):
        hits = hits + jnp.where(ids_t[r : r + 1, :] == expert, 1.0, 0.0)
    earlier = jnp.where(iota((tokens, tokens), 0) < iota((tokens, tokens), 1), 1.0, 0.0)
    before = dot(hits.astype(BF16), earlier.astype(BF16))
    return [jnp.where(before == s, hits, 0.0) for s in range(CAP)]


def send_kernel(*refs, with_p):
    if with_p:
        ids_ref, probs_ref, tok_ref, out_ref = refs
    else:
        ids_ref, tok_ref, out_ref = refs
    ids_t = ids_ref[...]
    group = tok_ref.shape[1] // QN
    live = live_tables(ids_t)
    q = iota(live[0].shape, 0) & (QN - 1)
    for s in range(CAP):
        total = jnp.zeros((LANES, group), F32)
        for k in range(QN):
            pick = jnp.where(q == k, live[s], 0.0).astype(BF16)
            total = total + dot(pick, tok_ref[:, k * group : (k + 1) * group])
        out_ref[:, s * group : (s + 1) * group] = total.astype(BF16)
    if with_p:
        expert = iota(live[0].shape, 0) >> 3
        probs = jnp.zeros(live[0].shape, F32)
        for r in range(ids_t.shape[0]):
            probs = probs + jnp.where(
                ids_t[r : r + 1, :] == expert, probs_ref[r : r + 1, :].astype(F32), 0.0
            )
        lane = iota((LANES, LANES), 1)
        tail = jnp.zeros((LANES, LANES), F32)
        for s in range(CAP):
            col = jnp.sum(live[s] * probs, axis=1, keepdims=True)
            tail = tail + jnp.where(lane == s, col, 0.0)
        out_ref[:, CAP * group :] = tail.astype(BF16)


def unpack_kernel(in_ref, out_ref, *, group):
    row, col = iota((LANES, LANES), 0), iota((LANES, LANES), 1)
    swap = jnp.where((row & 15) * QN + (row >> 4) == col, 1.0, 0.0).astype(BF16)
    for s in range(CAP):
        got = dot(swap, in_ref[:, s * group : (s + 1) * group]).astype(BF16)
        for k in range(QN):
            out_ref[s * 16 : (s + 1) * 16, k * group : (k + 1) * group] = got[
                k * 16 : (k + 1) * 16, :
            ]
    if out_ref.shape[1] > QN * group:
        tail = dot(swap, in_ref[:, CAP * group :])
        for s in range(CAP):
            out_ref[s * 16 : (s + 1) * 16, QN * group :] = jnp.broadcast_to(
                tail[0:16, s : s + 1], (16, LANES)
            ).astype(BF16)


BLOCKS = 4


def stacked(sources, target, sems, n):
    rows, width = sources[0].shape
    step = (width // BLOCKS) // LANES * LANES
    start = n * step
    size = step if n < BLOCKS - 1 else width - start
    return [
        pltpu.make_async_copy(
            a.at[:, pl.ds(start, size)],
            target.at[pl.ds(k * rows, rows), pl.ds(start, size)],
            sems.at[k * BLOCKS + n],
        )
        for k, a in enumerate(sources)
    ]


def ready(*copies):
    for group in copies:
        for c in group:
            c.wait()


def pre_kernel(*refs):
    xs, ws = refs[0:8], refs[8:12]
    gate_ref, up_ref, x_out, w_all, x_sems, w_sems = refs[12:]
    x_plan = [stacked(xs, x_out, x_sems, n) for n in range(BLOCKS)]
    w_plan = [stacked(ws, w_all, w_sems, n) for n in range(BLOCKS)]
    for n in range(BLOCKS):
        for c in w_plan[n] + x_plan[n]:
            c.start()
    step = x_out.shape[1] // BLOCKS
    half = w_all.shape[0] // 2
    for n in range(BLOCKS):
        ready(w_plan[n], x_plan[n])
        cols = slice(n * step, (n + 1) * step)
        for out_ref, first in ((gate_ref, 0), (up_ref, half)):
            got = dot_nt(w_all[first : first + half, cols], x_out[:, cols])
            if n == 0:
                out_ref[...] = got
            else:
                out_ref[...] += got


def main_kernel(*refs):
    ys, ds, ws, (gate_ref, up_ref) = refs[0:8], refs[8:10], refs[10:14], refs[14:16]
    outs, (dg_ref, du_ref, hid_ref, y_all) = refs[16:24], refs[24:28]
    d_all, w_all, acc, y_sems, d_sems, w_sems = refs[28:]
    y_plan = [stacked(ys, y_all, y_sems, n) for n in range(BLOCKS)]
    d_plan = [stacked(ds, d_all, d_sems, n) for n in range(BLOCKS)]
    w_plan = [stacked(ws, w_all, w_sems, n) for n in range(BLOCKS)]
    for n in range(BLOCKS):
        for c in d_plan[n] + y_plan[n]:
            c.start()
    for n in range(BLOCKS):
        for c in w_plan[n]:
            c.start()
    width, total = d_all.shape[1], y_all.shape[0]
    rows = total // 8
    step = width // BLOCKS
    for n in range(BLOCKS):
        ready(d_plan[n], y_plan[n])
        cols = slice(n * step, (n + 1) * step)
        got = dot_nt(d_all[:, cols], y_all[:, cols])
        if n == 0:
            acc[...] = got
        else:
            acc[...] += got
    back = acc[...]
    probs = y_all[:, width:].astype(F32)
    prob = jnp.transpose(probs)[0:1, :]
    gate, up = gate_ref[...], up_ref[...]
    sig = jax.nn.sigmoid(gate)
    hidden = gate * sig * up
    part = jnp.sum(hidden * back, axis=0, keepdims=True)
    scaled = prob * back
    d_gate = scaled * up * sig * (1.0 + gate * (1.0 - sig))
    d_up = scaled * gate * sig
    hid_ref[...] = hidden.astype(BF16)
    dg_ref[...] = d_gate.astype(BF16)
    du_ref[...] = d_up.astype(BF16)
    both = jnp.transpose(jnp.concatenate([d_gate, d_up], axis=0)).astype(BF16)
    high = part.astype(BF16).astype(F32)
    tail = jnp.where(
        iota((LANES, total), 0) < LANES // 2,
        jnp.broadcast_to(high, (LANES, total)),
        jnp.broadcast_to(part - high, (LANES, total)),
    )
    tail = jnp.transpose(tail).astype(BF16)
    for k in range(8):
        outs[k][:, width:] = tail[k * rows : (k + 1) * rows, :]
    for n in range(BLOCKS):
        ready(w_plan[n])
        for m in range(2):
            cols = slice(n * step + m * step // 2, n * step + (m + 1) * step // 2)
            got = dot(both, w_all[:, cols]).astype(BF16)
            for k in range(8):
                outs[k][:, cols] = got[k * rows : (k + 1) * rows, :]


def wgrad_kernel(hid_ref, dg_ref, du_ref, y_ref, prob_ref, x_ref, *rest, away):
    hid = hid_ref.shape[0] // 2
    first = hid if away else 0
    scaled = (prob_ref[:, 0:1].astype(F32) * y_ref[...].astype(F32)).astype(BF16)
    sides = ((dg_ref, x_ref[...]), (du_ref, x_ref[...]), (hid_ref, scaled))
    for i, (left, right) in enumerate(sides):
        total = dot(left[first : first + hid, :], right)
        if away:
            rest[0][i * hid : (i + 1) * hid, :] = total.astype(BF16)
        else:
            came = rest[0][i * hid : (i + 1) * hid, :].astype(F32)
            rest[1 + i][...] = (total + came).astype(BF16)


def summed(refs):
    total = refs[0][...].astype(F32)
    for r in refs[1:]:
        total = total + r[...].astype(F32)
    return total


def join_kernel(*refs, width):
    *parts, out_ref = refs
    body = [p.at[:, pl.ds(0, width)] for p in parts]
    out_ref[:, 0:width] = summed(body).astype(BF16)
    tail = summed([p.at[:, pl.ds(width, LANES)] for p in parts])
    value = tail[:, 0:1] + tail[:, LANES // 2 : LANES // 2 + 1]
    high = value.astype(BF16).astype(F32)
    out_ref[:, width:] = jnp.where(
        iota(tail.shape, 1) < LANES // 2, high, value - high
    ).astype(BF16)


def last_kernel(*refs, group):
    *parts, out_ref = refs
    width = QN * group
    row, col = iota((LANES, LANES), 0), iota((LANES, LANES), 1)
    swap = jnp.where((col & 15) * QN + (col >> 4) == row, 1.0, 0.0).astype(BF16)
    total = summed([p.at[:, pl.ds(0, width)] for p in parts]).astype(BF16)
    for s in range(CAP):
        stack = jnp.concatenate(
            [total[s * 16 : (s + 1) * 16, k * group : (k + 1) * group] for k in range(QN)], axis=0
        )
        out_ref[:, s * group : (s + 1) * group] = dot(swap, stack).astype(BF16)
    tail = summed([p.at[:, pl.ds(width, LANES)] for p in parts])
    value = tail[:, 0:1] + tail[:, LANES // 2 : LANES // 2 + 1]
    lane = iota((16, LANES), 1)
    cols = jnp.zeros((16, LANES), F32)
    for s in range(CAP):
        cols = cols + jnp.where(lane == s, value[s * 16 : (s + 1) * 16, :], 0.0)
    stack = jnp.concatenate([cols] * QN, axis=0).astype(BF16)
    out_ref[:, CAP * group :] = dot(swap, stack).astype(BF16)


def final_kernel(ids_ref, in_ref, tok_ref, gate_ref, *, group):
    ids_t = ids_ref[...]
    live = live_tables(ids_t)
    lane = iota(live[0].shape, 1)
    sides = [jnp.transpose(v) for v in live]
    for k in range(QN):
        total = jnp.zeros((live[0].shape[1], group), F32)
        for s in range(CAP):
            pick = jnp.where((lane & (QN - 1)) == k, sides[s], 0.0).astype(BF16)
            total = total + dot(pick, in_ref[:, s * group : (s + 1) * group])
        tok_ref[:, k * group : (k + 1) * group] = total.astype(BF16)
    row = iota(live[0].shape, 0)
    value = jnp.zeros(live[0].shape, F32)
    for s in range(CAP):
        col = in_ref[:, CAP * group + s : CAP * group + s + 1].astype(F32)
        value = value + live[s] * col
    value = jnp.where((row & (QN - 1)) == 0, value, 0.0)
    for r in range(ids_t.shape[0]):
        mine = jnp.where(ids_t[r : r + 1, :] == (row >> 3), value, 0.0)
        gate_ref[r : r + 1, :] = jnp.sum(mine, axis=0, keepdims=True).astype(BF16)


def per_device(tokens, cotangent, gate_probs, expert_ids, w_gate, w_up, w_down):
    width = tokens.shape[1]
    group = width // QN
    wide = width + LANES
    rows = CAP * 16
    total = 8 * rows
    g, u, d = w_gate[0], w_up[0], w_down[0]
    hid = g.shape[0]
    ids_t, probs_t = expert_ids.T, gate_probs.T
    shape = jax.ShapeDtypeStruct
    any_spec, vmem = pl.BlockSpec(memory_space=pl.ANY), pl.BlockSpec(memory_space=pltpu.VMEM)
    dma = pltpu.SemaphoreType.DMA
    together = lax.optimization_barrier
    work = 2 * total * width * 2 * hid

    def exchange(a):
        a = a.reshape(16, QN, a.shape[1])
        a = lax.all_to_all(a, "ep", split_axis=0, concat_axis=0, tiled=True)
        return a.reshape(LANES, a.shape[2])

    def unpack(a, columns, name):
        return call(
            functools.partial(unpack_kernel, group=group),
            shape((rows, columns), BF16),
            name,
            cost=(10**8, 10**6),
        )(a)

    send_x = call(
        functools.partial(send_kernel, with_p=False),
        shape((LANES, CAP * group), BF16),
        "send_x",
        cost=(6 * 10**8, 2 * 10**6),
    )(ids_t, tokens)
    core_g, core_u, core_d = hop(g, C_SWAP), hop(u, C_SWAP), hop(d, C_SWAP)
    got_x, core_g, core_u, core_d = together((exchange(send_x), core_g, core_u, core_d))
    x = unpack(got_x, width, "unpack_x")
    xa, xb, oth = hop(x, X_A), hop(x, X_B), hop(x, Z_SWAP)
    send_y = call(
        functools.partial(send_kernel, with_p=True),
        shape((LANES, CAP * group + LANES), BF16),
        "send_y",
        cost=(6 * 10**8, 2 * 10**6),
    )(ids_t, probs_t, cotangent)
    send_y, x_now = together((send_y, x))
    got_y = exchange(send_y)
    xa, xb, oth = together((xa, xb, oth))
    ob, oa, far = hop(oth, X_B), hop(xa, Z_SWAP), hop(xa, X_A)
    o_far = hop(ob, X_B)
    far, oa, ob, got_y = together((far, oa, ob, got_y))
    y = unpack(got_y, wide, "unpack_y")
    ya, yb, y_oth = hop(y, X_A), hop(y, X_B), hop(y, Z_SWAP)
    ya, yb, y_oth, o_far = together((ya, yb, y_oth, o_far))
    yob, yoa, y_far = hop(y_oth, X_B), hop(ya, Z_SWAP), hop(ya, X_A)
    yo_far = hop(yob, X_B)
    gate, up, x_all = call(
        pre_kernel,
        [shape((2 * hid, total), F32)] * 2 + [shape((total, width), BF16)],
        "pre",
        scratch=[pltpu.VMEM((4 * hid, width), BF16), dma((32,)), dma((16,))],
        specs=[any_spec] * 12,
        cost=(2 * work, 10 * 10**6),
    )(x, xa, far, xb, oth, oa, o_far, ob, g, core_g, u, core_u)
    *parts, d_gate, d_up, hidden, y_all = call(
        main_kernel,
        [shape((rows, wide), BF16)] * 8
        + [shape((2 * hid, total), BF16)] * 3
        + [shape((total, wide), BF16)],
        "main",
        scratch=[
            pltpu.VMEM((2 * hid, width), BF16),
            pltpu.VMEM((4 * hid, width), BF16),
            pltpu.VMEM((2 * hid, total), F32),
            dma((32,)),
            dma((8,)),
            dma((16,)),
        ],
        specs=[any_spec] * 14 + [vmem] * 2,
        cost=(3 * work, 14 * 10**6),
    )(
        *(y, ya, y_far, yb, y_oth, yoa, yo_far, yob),
        *(d, core_d, g, core_g, u, core_u, gate, up),
    )

    blocks = 4

    def wgrad(*came):
        cols = width // blocks

        def part(height):
            return pl.BlockSpec((height, cols), lambda n: (0, n))

        prob = pl.BlockSpec((total, LANES), lambda n: (0, width // LANES))
        left = pl.BlockSpec((2 * hid, total), lambda n: (0, 0))
        out = [shape((hid, width), BF16)] * 3 if came else shape((3 * hid, width), BF16)
        return pl.pallas_call(
            functools.partial(wgrad_kernel, away=not came),
            out_shape=out,
            grid=(blocks,),
            in_specs=[left] * 3
            + [part(total), prob, part(total)]
            + [part(3 * hid)] * len(came),
            out_specs=[part(hid)] * 3 if came else part(3 * hid),
            compiler_params=pltpu.CompilerParams(vmem_limit_bytes=32 * 1024 * 1024),
            name="wgrad_mine" if came else "wgrad_away",
            cost_estimate=pl.CostEstimate(
                flops=work * 3 // 2, bytes_accessed=12 * 10**6, transcendentals=0
            ),
        )(hidden, d_gate, d_up, y_all, y_all, x_all, *came)

    def join(*a):
        return call(
            functools.partial(join_kernel, width=width),
            shape((rows, wide), BF16),
            "join",
            cost=(10**6, 10**6),
        )(*a)

    own, pa, far, pb, oth, oa, o_far, ob = parts
    of, oa, ob = hop(o_far, Z_SWAP), hop(oa, X_B), hop(ob, X_A)
    away = wgrad()
    of, oa, ob, pb, away = together((of, oa, ob, pb, away))
    f, oz = hop(join(far, of), X_B), hop(join(oth, oa, ob), Z_SWAP)
    pb = hop(pb, X_A)
    f, oz, pb, away = together((f, oz, pb, away))
    pa = hop(join(pa, f), X_B)
    came = hop(away, C_SWAP)
    last = call(
        functools.partial(last_kernel, group=group),
        shape((LANES, CAP * group + LANES), BF16),
        "last",
        cost=(10**8, 3 * 10**6),
    )(own, pa, pb, oz)
    last, hidden = together((last, hidden))
    back = exchange(last)
    g_grad, u_grad, d_grad = wgrad(came)
    back, g_grad, u_grad, d_grad = together((back, g_grad, u_grad, d_grad))
    token_grad, gate_t = call(
        functools.partial(final_kernel, group=group),
        [shape(tokens.shape, BF16), shape(ids_t.shape, BF16)],
        "final",
        cost=(6 * 10**8, 2 * 10**6),
    )(ids_t, back)
    return (token_grad, gate_t.T, g_grad[None], u_grad[None], d_grad[None])


def solution(mesh):
    tok = P(("edp", "ep"), None)
    wgt = P("ep", "edp", None)
    return jax.shard_map(
        per_device,
        mesh=mesh,
        in_specs=(tok, tok, tok, tok, wgt, wgt, wgt),
        out_specs=(tok, tok, wgt, wgt, wgt),
        check_vma=False,
    )
```

```python
import functools

import jax
import jax.numpy as jnp
from jax import lax
from jax.experimental import pallas as pl
from jax.experimental.pallas import tpu as pltpu
from jax.sharding import PartitionSpec as P

CAP = 3
QN = 8
LANES = 128
F32 = jnp.float32
BF16 = jnp.bfloat16


def x_perm(step):
    pairs = []
    for i in range(16):
        x = ((i >> 1) + (step if i % 2 == 0 else -step)) & 3
        pairs.append((i, (i & 9) | (x << 1)))
    return pairs


X_A, X_B = x_perm(1), x_perm(-1)
Z_SWAP = [(i, i ^ 8) for i in range(16)]
C_SWAP = [(i, i ^ 1) for i in range(16)]


def hop(a, perm):
    return lax.ppermute(a, "edp", perm)


def iota(shape, dim):
    return lax.broadcasted_iota(jnp.int32, shape, dim)


def dot(a, b):
    return jnp.dot(a, b, preferred_element_type=F32)


def dot_nt(a, b):
    return lax.dot_general(a, b, (((1,), (1,)), ((), ())), preferred_element_type=F32)


def call(kernel, outs, name, scratch=(), specs=None, out_specs=None, cost=None, limit=48):
    one = pl.BlockSpec(memory_space=pltpu.VMEM)
    params = pltpu.CompilerParams(vmem_limit_bytes=limit * 1024 * 1024)

    def run(*args):
        return pl.pallas_call(
            kernel,
            out_shape=outs,
            in_specs=[one] * len(args) if specs is None else specs,
            out_specs=jax.tree.map(lambda _: one, outs) if out_specs is None else out_specs,
            scratch_shapes=scratch,
            compiler_params=params,
            name=name,
            cost_estimate=cost
            and pl.CostEstimate(flops=cost[0], bytes_accessed=cost[1], transcendentals=0),
        )(*args)

    return run


def live_tables(ids_t):
    tokens = ids_t.shape[1]
    expert = iota((LANES, tokens), 0) >> 3
    hits = jnp.zeros((LANES, tokens), F32)
    for r in range(ids_t.shape[0]):
        hits = hits + jnp.where(ids_t[r : r + 1, :] == expert, 1.0, 0.0)
    earlier = jnp.where(iota((tokens, tokens), 0) < iota((tokens, tokens), 1), 1.0, 0.0)
    before = dot(hits.astype(BF16), earlier.astype(BF16))
    return [jnp.where(before == s, hits, 0.0) for s in range(CAP)]


def send_kernel(*refs, with_p):
    if with_p:
        ids_ref, probs_ref, tok_ref, out_ref = refs
    else:
        ids_ref, tok_ref, out_ref = refs
    ids_t = ids_ref[...]
    group = tok_ref.shape[1] // QN
    live = live_tables(ids_t)
    q = iota(live[0].shape, 0) & (QN - 1)
    for s in range(CAP):
        total = jnp.zeros((LANES, group), F32)
        for k in range(QN):
            pick = jnp.where(q == k, live[s], 0.0).astype(BF16)
            total = total + dot(pick, tok_ref[:, k * group : (k + 1) * group])
        out_ref[:, s * group : (s + 1) * group] = total.astype(BF16)
    if with_p:
        expert = iota(live[0].shape, 0) >> 3
        probs = jnp.zeros(live[0].shape, F32)
        for r in range(ids_t.shape[0]):
            probs = probs + jnp.where(
                ids_t[r : r + 1, :] == expert, probs_ref[r : r + 1, :].astype(F32), 0.0
            )
        lane = iota((LANES, LANES), 1)
        tail = jnp.zeros((LANES, LANES), F32)
        for s in range(CAP):
            col = jnp.sum(live[s] * probs, axis=1, keepdims=True)
            tail = tail + jnp.where(lane == s, col, 0.0)
        out_ref[:, CAP * group :] = tail.astype(BF16)


def unpack_kernel(in_ref, out_ref, *, group):
    row, col = iota((LANES, LANES), 0), iota((LANES, LANES), 1)
    swap = jnp.where((row & 15) * QN + (row >> 4) == col, 1.0, 0.0).astype(BF16)
    for s in range(CAP):
        got = dot(swap, in_ref[:, s * group : (s + 1) * group]).astype(BF16)
        for k in range(QN):
            out_ref[s * 16 : (s + 1) * 16, k * group : (k + 1) * group] = got[
                k * 16 : (k + 1) * 16, :
            ]
    if out_ref.shape[1] > QN * group:
        tail = dot(swap, in_ref[:, CAP * group :])
        for s in range(CAP):
            out_ref[s * 16 : (s + 1) * 16, QN * group :] = jnp.broadcast_to(
                tail[0:16, s : s + 1], (16, LANES)
            ).astype(BF16)


BLOCKS = 4


def stacked(sources, target, sems, n):
    rows, width = sources[0].shape
    step = (width // BLOCKS) // LANES * LANES
    start = n * step
    size = step if n < BLOCKS - 1 else width - start
    return [
        pltpu.make_async_copy(
            a.at[:, pl.ds(start, size)],
            target.at[pl.ds(k * rows, rows), pl.ds(start, size)],
            sems.at[k * BLOCKS + n],
        )
        for k, a in enumerate(sources)
    ]


def ready(*copies):
    for group in copies:
        for c in group:
            c.wait()


def pre_kernel(*refs):
    xs, ws = refs[0:8], refs[8:12]
    gate_ref, up_ref, x_out, w_all, x_sems, w_sems = refs[12:]
    x_plan = [stacked(xs, x_out, x_sems, n) for n in range(BLOCKS)]
    w_plan = [stacked(ws, w_all, w_sems, n) for n in range(BLOCKS)]
    for n in range(BLOCKS):
        for c in w_plan[n] + x_plan[n]:
            c.start()
    step = x_out.shape[1] // BLOCKS
    half = w_all.shape[0] // 2
    for n in range(BLOCKS):
        ready(w_plan[n], x_plan[n])
        cols = slice(n * step, (n + 1) * step)
        for out_ref, first in ((gate_ref, 0), (up_ref, half)):
            got = dot_nt(w_all[first : first + half, cols], x_out[:, cols])
            if n == 0:
                out_ref[...] = got
            else:
                out_ref[...] += got


def main_kernel(*refs):
    ys, ds, ws, (gate_ref, up_ref) = refs[0:8], refs[8:10], refs[10:14], refs[14:16]
    outs, (dg_ref, du_ref, hid_ref, y_all) = refs[16:24], refs[24:28]
    d_all, w_all, acc, y_sems, d_sems, w_sems = refs[28:]
    y_plan = [stacked(ys, y_all, y_sems, n) for n in range(BLOCKS)]
    d_plan = [stacked(ds, d_all, d_sems, n) for n in range(BLOCKS)]
    w_plan = [stacked(ws, w_all, w_sems, n) for n in range(BLOCKS)]
    for n in range(BLOCKS):
        for c in d_plan[n] + y_plan[n]:
            c.start()
    for n in range(BLOCKS):
        for c in w_plan[n]:
            c.start()
    width, total = d_all.shape[1], y_all.shape[0]
    rows = total // 8
    step = width // BLOCKS
    for n in range(BLOCKS):
        ready(d_plan[n], y_plan[n])
        cols = slice(n * step, (n + 1) * step)
        got = dot_nt(d_all[:, cols], y_all[:, cols])
        if n == 0:
            acc[...] = got
        else:
            acc[...] += got
    back = acc[...]
    probs = y_all[:, width:].astype(F32)
    prob = jnp.transpose(probs)[0:1, :]
    gate, up = gate_ref[...], up_ref[...]
    sig = jax.nn.sigmoid(gate)
    hidden = gate * sig * up
    part = jnp.sum(hidden * back, axis=0, keepdims=True)
    scaled = prob * back
    d_gate = scaled * up * sig * (1.0 + gate * (1.0 - sig))
    d_up = scaled * gate * sig
    hid_ref[...] = hidden.astype(BF16)
    dg_ref[...] = d_gate.astype(BF16)
    du_ref[...] = d_up.astype(BF16)
    both = jnp.transpose(jnp.concatenate([d_gate, d_up], axis=0)).astype(BF16)
    high = part.astype(BF16).astype(F32)
    tail = jnp.where(
        iota((LANES, total), 0) < LANES // 2,
        jnp.broadcast_to(high, (LANES, total)),
        jnp.broadcast_to(part - high, (LANES, total)),
    )
    tail = jnp.transpose(tail).astype(BF16)
    for k in range(8):
        outs[k][:, width:] = tail[k * rows : (k + 1) * rows, :]
    for n in range(BLOCKS):
        ready(w_plan[n])
        for m in range(2):
            cols = slice(n * step + m * step // 2, n * step + (m + 1) * step // 2)
            got = dot(both, w_all[:, cols]).astype(BF16)
            for k in range(8):
                outs[k][:, cols] = got[k * rows : (k + 1) * rows, :]


def wgrad_kernel(hid_ref, dg_ref, du_ref, y_ref, prob_ref, x_ref, *rest, away):
    hid = hid_ref.shape[0] // 2
    first = hid if away else 0
    scaled = (prob_ref[:, 0:1].astype(F32) * y_ref[...].astype(F32)).astype(BF16)
    sides = ((dg_ref, x_ref[...]), (du_ref, x_ref[...]), (hid_ref, scaled))
    for i, (left, right) in enumerate(sides):
        total = dot(left[first : first + hid, :], right)
        if away:
            rest[0][i * hid : (i + 1) * hid, :] = total.astype(BF16)
        else:
            came = rest[0][i * hid : (i + 1) * hid, :].astype(F32)
            rest[1 + i][...] = (total + came).astype(BF16)


def summed(refs):
    total = refs[0][...].astype(F32)
    for r in refs[1:]:
        total = total + r[...].astype(F32)
    return total


def join_kernel(*refs, width):
    *parts, out_ref = refs
    body = [p.at[:, pl.ds(0, width)] for p in parts]
    out_ref[:, 0:width] = summed(body).astype(BF16)
    tail = summed([p.at[:, pl.ds(width, LANES)] for p in parts])
    value = tail[:, 0:1] + tail[:, LANES // 2 : LANES // 2 + 1]
    high = value.astype(BF16).astype(F32)
    out_ref[:, width:] = jnp.where(
        iota(tail.shape, 1) < LANES // 2, high, value - high
    ).astype(BF16)


def last_kernel(*refs, group):
    *parts, out_ref = refs
    width = QN * group
    row, col = iota((LANES, LANES), 0), iota((LANES, LANES), 1)
    swap = jnp.where((col & 15) * QN + (col >> 4) == row, 1.0, 0.0).astype(BF16)
    total = summed([p.at[:, pl.ds(0, width)] for p in parts]).astype(BF16)
    for s in range(CAP):
        stack = jnp.concatenate(
            [total[s * 16 : (s + 1) * 16, k * group : (k + 1) * group] for k in range(QN)], axis=0
        )
        out_ref[:, s * group : (s + 1) * group] = dot(swap, stack).astype(BF16)
    tail = summed([p.at[:, pl.ds(width, LANES)] for p in parts])
    value = tail[:, 0:1] + tail[:, LANES // 2 : LANES // 2 + 1]
    lane = iota((16, LANES), 1)
    cols = jnp.zeros((16, LANES), F32)
    for s in range(CAP):
        cols = cols + jnp.where(lane == s, value[s * 16 : (s + 1) * 16, :], 0.0)
    stack = jnp.concatenate([cols] * QN, axis=0).astype(BF16)
    out_ref[:, CAP * group :] = dot(swap, stack).astype(BF16)


def final_kernel(ids_ref, in_ref, tok_ref, gate_ref, *, group):
    ids_t = ids_ref[...]
    live = live_tables(ids_t)
    lane = iota(live[0].shape, 1)
    sides = [jnp.transpose(v) for v in live]
    for k in range(QN):
        total = jnp.zeros((live[0].shape[1], group), F32)
        for s in range(CAP):
            pick = jnp.where((lane & (QN - 1)) == k, sides[s], 0.0).astype(BF16)
            total = total + dot(pick, in_ref[:, s * group : (s + 1) * group])
        tok_ref[:, k * group : (k + 1) * group] = total.astype(BF16)
    row = iota(live[0].shape, 0)
    value = jnp.zeros(live[0].shape, F32)
    for s in range(CAP):
        col = in_ref[:, CAP * group + s : CAP * group + s + 1].astype(F32)
        value = value + live[s] * col
    value = jnp.where((row & (QN - 1)) == 0, value, 0.0)
    for r in range(ids_t.shape[0]):
        mine = jnp.where(ids_t[r : r + 1, :] == (row >> 3), value, 0.0)
        gate_ref[r : r + 1, :] = jnp.sum(mine, axis=0, keepdims=True).astype(BF16)


def per_device(tokens, cotangent, gate_probs, expert_ids, w_gate, w_up, w_down):
    width = tokens.shape[1]
    group = width // QN
    wide = width + LANES
    rows = CAP * 16
    total = 8 * rows
    g, u, d = w_gate[0], w_up[0], w_down[0]
    hid = g.shape[0]
    ids_t, probs_t = expert_ids.T, gate_probs.T
    shape = jax.ShapeDtypeStruct
    any_spec, vmem = pl.BlockSpec(memory_space=pl.ANY), pl.BlockSpec(memory_space=pltpu.VMEM)
    dma = pltpu.SemaphoreType.DMA
    together = lax.optimization_barrier
    work = 2 * total * width * 2 * hid

    def exchange(a):
        a = a.reshape(16, QN, a.shape[1])
        a = lax.all_to_all(a, "ep", split_axis=0, concat_axis=0, tiled=True)
        return a.reshape(LANES, a.shape[2])

    def unpack(a, columns, name):
        return call(
            functools.partial(unpack_kernel, group=group),
            shape((rows, columns), BF16),
            name,
            cost=(10**8, 10**6),
        )(a)

    send_x = call(
        functools.partial(send_kernel, with_p=False),
        shape((LANES, CAP * group), BF16),
        "send_x",
        cost=(6 * 10**8, 2 * 10**6),
    )(ids_t, tokens)
    core_g, core_u, core_d = hop(g, C_SWAP), hop(u, C_SWAP), hop(d, C_SWAP)
    got_x, core_g, core_u, core_d = together((exchange(send_x), core_g, core_u, core_d))
    x = unpack(got_x, width, "unpack_x")
    xa, xb, oth = hop(x, X_A), hop(x, X_B), hop(x, Z_SWAP)
    send_y = call(
        functools.partial(send_kernel, with_p=True),
        shape((LANES, CAP * group + LANES), BF16),
        "send_y",
        cost=(6 * 10**8, 2 * 10**6),
    )(ids_t, probs_t, cotangent)
    send_y, x_now = together((send_y, x))
    got_y = exchange(send_y)
    xa, xb, oth = together((xa, xb, oth))
    ob, oa, far = hop(oth, X_B), hop(oth, X_A), hop(xa, X_A)
    o_far = hop(ob, X_B)
    far, oa, ob, got_y = together((far, oa, ob, got_y))
    y = unpack(got_y, wide, "unpack_y")
    ya, yb, y_oth = hop(y, X_A), hop(y, X_B), hop(y, Z_SWAP)
    ya, yb, y_oth = together((ya, yb, y_oth))
    yob, yoa, y_far = hop(y_oth, X_B), hop(ya, Z_SWAP), hop(ya, X_A)
    yo_far = hop(yob, X_B)
    gate, up, x_all = call(
        pre_kernel,
        [shape((2 * hid, total), F32)] * 2 + [shape((total, width), BF16)],
        "pre",
        scratch=[pltpu.VMEM((4 * hid, width), BF16), dma((32,)), dma((16,))],
        specs=[any_spec] * 12,
        cost=(2 * work, 10 * 10**6),
    )(x, xa, far, xb, oth, oa, o_far, ob, g, core_g, u, core_u)
    *parts, d_gate, d_up, hidden, y_all = call(
        main_kernel,
        [shape((rows, wide), BF16)] * 8
        + [shape((2 * hid, total), BF16)] * 3
        + [shape((total, wide), BF16)],
        "main",
        scratch=[
            pltpu.VMEM((2 * hid, width), BF16),
            pltpu.VMEM((4 * hid, width), BF16),
            pltpu.VMEM((2 * hid, total), F32),
            dma((32,)),
            dma((8,)),
            dma((16,)),
        ],
        specs=[any_spec] * 14 + [vmem] * 2,
        cost=(3 * work, 14 * 10**6),
    )(
        *(y, ya, y_far, yb, y_oth, yoa, yo_far, yob),
        *(d, core_d, g, core_g, u, core_u, gate, up),
    )

    blocks = 4

    def wgrad(*came):
        cols = width // blocks

        def part(height):
            return pl.BlockSpec((height, cols), lambda n: (0, n))

        prob = pl.BlockSpec((total, LANES), lambda n: (0, width // LANES))
        left = pl.BlockSpec((2 * hid, total), lambda n: (0, 0))
        out = [shape((hid, width), BF16)] * 3 if came else shape((3 * hid, width), BF16)
        return pl.pallas_call(
            functools.partial(wgrad_kernel, away=not came),
            out_shape=out,
            grid=(blocks,),
            in_specs=[left] * 3
            + [part(total), prob, part(total)]
            + [part(3 * hid)] * len(came),
            out_specs=[part(hid)] * 3 if came else part(3 * hid),
            compiler_params=pltpu.CompilerParams(vmem_limit_bytes=32 * 1024 * 1024),
            name="wgrad_mine" if came else "wgrad_away",
            cost_estimate=pl.CostEstimate(
                flops=work * 3 // 2, bytes_accessed=12 * 10**6, transcendentals=0
            ),
        )(hidden, d_gate, d_up, y_all, y_all, x_all, *came)

    def join(*a):
        return call(
            functools.partial(join_kernel, width=width),
            shape((rows, wide), BF16),
            "join",
            cost=(10**6, 10**6),
        )(*a)

    own, pa, far, pb, oth, oa, o_far, ob = parts
    of, oa, ob = hop(o_far, Z_SWAP), hop(oa, X_B), hop(ob, X_A)
    away = wgrad()
    of, oa, ob, pb, away = together((of, oa, ob, pb, away))
    f, oz = hop(join(far, of), X_B), hop(join(oth, oa, ob), Z_SWAP)
    pb = hop(pb, X_A)
    f, oz, pb, away = together((f, oz, pb, away))
    pa = hop(join(pa, f), X_B)
    came = hop(away, C_SWAP)
    last = call(
        functools.partial(last_kernel, group=group),
        shape((LANES, CAP * group + LANES), BF16),
        "last",
        cost=(10**8, 3 * 10**6),
    )(own, pa, pb, oz)
    last, hidden = together((last, hidden))
    back = exchange(last)
    g_grad, u_grad, d_grad = wgrad(came)
    back, g_grad, u_grad, d_grad = together((back, g_grad, u_grad, d_grad))
    token_grad, gate_t = call(
        functools.partial(final_kernel, group=group),
        [shape(tokens.shape, BF16), shape(ids_t.shape, BF16)],
        "final",
        cost=(6 * 10**8, 2 * 10**6),
    )(ids_t, back)
    return (token_grad, gate_t.T, g_grad[None], u_grad[None], d_grad[None])


def solution(mesh):
    tok = P(("edp", "ep"), None)
    wgt = P("ep", "edp", None)
    return jax.shard_map(
        per_device,
        mesh=mesh,
        in_specs=(tok, tok, tok, tok, wgt, wgt, wgt),
        out_specs=(tok, tok, wgt, wgt, wgt),
        check_vma=False,
    )
```

```python
import functools

import jax
import jax.numpy as jnp
from jax import lax
from jax.experimental import pallas as pl
from jax.experimental.pallas import tpu as pltpu
from jax.sharding import PartitionSpec as P

CAP = 3
QN = 8
LANES = 128
F32 = jnp.float32
BF16 = jnp.bfloat16


def x_perm(step):
    pairs = []
    for i in range(16):
        x = ((i >> 1) + (step if i % 2 == 0 else -step)) & 3
        pairs.append((i, (i & 9) | (x << 1)))
    return pairs


X_A, X_B = x_perm(1), x_perm(-1)
Z_SWAP = [(i, i ^ 8) for i in range(16)]
C_SWAP = [(i, i ^ 1) for i in range(16)]


def hop(a, perm):
    return lax.ppermute(a, "edp", perm)


def iota(shape, dim):
    return lax.broadcasted_iota(jnp.int32, shape, dim)


def dot(a, b):
    return jnp.dot(a, b, preferred_element_type=F32)


def dot_nt(a, b):
    return lax.dot_general(a, b, (((1,), (1,)), ((), ())), preferred_element_type=F32)


def call(kernel, outs, name, scratch=(), specs=None, out_specs=None, cost=None, limit=48):
    one = pl.BlockSpec(memory_space=pltpu.VMEM)
    params = pltpu.CompilerParams(vmem_limit_bytes=limit * 1024 * 1024)

    def run(*args):
        return pl.pallas_call(
            kernel,
            out_shape=outs,
            in_specs=[one] * len(args) if specs is None else specs,
            out_specs=jax.tree.map(lambda _: one, outs) if out_specs is None else out_specs,
            scratch_shapes=scratch,
            compiler_params=params,
            name=name,
            cost_estimate=cost
            and pl.CostEstimate(flops=cost[0], bytes_accessed=cost[1], transcendentals=0),
        )(*args)

    return run


def live_tables(ids_t):
    tokens = ids_t.shape[1]
    expert = iota((LANES, tokens), 0) >> 3
    hits = jnp.zeros((LANES, tokens), F32)
    for r in range(ids_t.shape[0]):
        hits = hits + jnp.where(ids_t[r : r + 1, :] == expert, 1.0, 0.0)
    earlier = jnp.where(iota((tokens, tokens), 0) < iota((tokens, tokens), 1), 1.0, 0.0)
    before = dot(hits.astype(BF16), earlier.astype(BF16))
    return [jnp.where(before == s, hits, 0.0) for s in range(CAP)]


def send_kernel(*refs, with_p):
    if with_p:
        ids_ref, probs_ref, tok_ref, out_ref = refs
    else:
        ids_ref, tok_ref, out_ref = refs
    ids_t = ids_ref[...]
    group = tok_ref.shape[1] // QN
    live = live_tables(ids_t)
    q = iota(live[0].shape, 0) & (QN - 1)
    for s in range(CAP):
        total = jnp.zeros((LANES, group), F32)
        for k in range(QN):
            pick = jnp.where(q == k, live[s], 0.0).astype(BF16)
            total = total + dot(pick, tok_ref[:, k * group : (k + 1) * group])
        out_ref[:, s * group : (s + 1) * group] = total.astype(BF16)
    if with_p:
        expert = iota(live[0].shape, 0) >> 3
        probs = jnp.zeros(live[0].shape, F32)
        for r in range(ids_t.shape[0]):
            probs = probs + jnp.where(
                ids_t[r : r + 1, :] == expert, probs_ref[r : r + 1, :].astype(F32), 0.0
            )
        lane = iota((LANES, LANES), 1)
        tail = jnp.zeros((LANES, LANES), F32)
        for s in range(CAP):
            col = jnp.sum(live[s] * probs, axis=1, keepdims=True)
            tail = tail + jnp.where(lane == s, col, 0.0)
        out_ref[:, CAP * group :] = tail.astype(BF16)


def unpack_kernel(in_ref, out_ref, *, group):
    row, col = iota((LANES, LANES), 0), iota((LANES, LANES), 1)
    swap = jnp.where((row & 15) * QN + (row >> 4) == col, 1.0, 0.0).astype(BF16)
    for s in range(CAP):
        got = dot(swap, in_ref[:, s * group : (s + 1) * group]).astype(BF16)
        for k in range(QN):
            out_ref[s * 16 : (s + 1) * 16, k * group : (k + 1) * group] = got[
                k * 16 : (k + 1) * 16, :
            ]
    if out_ref.shape[1] > QN * group:
        tail = dot(swap, in_ref[:, CAP * group :])
        for s in range(CAP):
            out_ref[s * 16 : (s + 1) * 16, QN * group :] = jnp.broadcast_to(
                tail[0:16, s : s + 1], (16, LANES)
            ).astype(BF16)


BLOCKS = 4


def stacked(sources, target, sems, n):
    rows, width = sources[0].shape
    step = (width // BLOCKS) // LANES * LANES
    start = n * step
    size = step if n < BLOCKS - 1 else width - start
    return [
        pltpu.make_async_copy(
            a.at[:, pl.ds(start, size)],
            target.at[pl.ds(k * rows, rows), pl.ds(start, size)],
            sems.at[k * BLOCKS + n],
        )
        for k, a in enumerate(sources)
    ]


def ready(*copies):
    for group in copies:
        for c in group:
            c.wait()


def pre_kernel(*refs):
    xs, ws = refs[0:8], refs[8:12]
    gate_ref, up_ref, x_out, w_all, x_sems, w_sems = refs[12:]
    x_plan = [stacked(xs, x_out, x_sems, n) for n in range(BLOCKS)]
    w_plan = [stacked(ws, w_all, w_sems, n) for n in range(BLOCKS)]
    for n in range(BLOCKS):
        for c in w_plan[n] + x_plan[n]:
            c.start()
    step = x_out.shape[1] // BLOCKS
    half = w_all.shape[0] // 2
    for n in range(BLOCKS):
        ready(w_plan[n], x_plan[n])
        cols = slice(n * step, (n + 1) * step)
        for out_ref, first in ((gate_ref, 0), (up_ref, half)):
            got = dot_nt(w_all[first : first + half, cols], x_out[:, cols])
            if n == 0:
                out_ref[...] = got
            else:
                out_ref[...] += got


def main_kernel(*refs):
    ys, ds, ws, (gate_ref, up_ref) = refs[0:8], refs[8:10], refs[10:14], refs[14:16]
    outs, (dg_ref, du_ref, hid_ref, y_all) = refs[16:24], refs[24:28]
    d_all, w_all, acc, y_sems, d_sems, w_sems = refs[28:]
    y_plan = [stacked(ys, y_all, y_sems, n) for n in range(BLOCKS)]
    d_plan = [stacked(ds, d_all, d_sems, n) for n in range(BLOCKS)]
    w_plan = [stacked(ws, w_all, w_sems, n) for n in range(BLOCKS)]
    for n in range(BLOCKS):
        for c in d_plan[n] + y_plan[n]:
            c.start()
    for n in range(BLOCKS):
        for c in w_plan[n]:
            c.start()
    width, total = d_all.shape[1], y_all.shape[0]
    rows = total // 8
    step = width // BLOCKS
    for n in range(BLOCKS):
        ready(d_plan[n], y_plan[n])
        cols = slice(n * step, (n + 1) * step)
        got = dot_nt(d_all[:, cols], y_all[:, cols])
        if n == 0:
            acc[...] = got
        else:
            acc[...] += got
    back = acc[...]
    probs = y_all[:, width:].astype(F32)
    prob = jnp.transpose(probs)[0:1, :]
    gate, up = gate_ref[...], up_ref[...]
    sig = jax.nn.sigmoid(gate)
    hidden = gate * sig * up
    part = jnp.sum(hidden * back, axis=0, keepdims=True)
    scaled = prob * back
    d_gate = scaled * up * sig * (1.0 + gate * (1.0 - sig))
    d_up = scaled * gate * sig
    hid_ref[...] = hidden.astype(BF16)
    dg_ref[...] = d_gate.astype(BF16)
    du_ref[...] = d_up.astype(BF16)
    both = jnp.transpose(jnp.concatenate([d_gate, d_up], axis=0)).astype(BF16)
    high = part.astype(BF16).astype(F32)
    tail = jnp.where(
        iota((LANES, total), 0) < LANES // 2,
        jnp.broadcast_to(high, (LANES, total)),
        jnp.broadcast_to(part - high, (LANES, total)),
    )
    tail = jnp.transpose(tail).astype(BF16)
    for k in range(8):
        outs[k][:, width:] = tail[k * rows : (k + 1) * rows, :]
    for n in range(BLOCKS):
        ready(w_plan[n])
        for m in range(2):
            cols = slice(n * step + m * step // 2, n * step + (m + 1) * step // 2)
            got = dot(both, w_all[:, cols]).astype(BF16)
            for k in range(8):
                outs[k][:, cols] = got[k * rows : (k + 1) * rows, :]


def wgrad_kernel(hid_ref, dg_ref, du_ref, y_ref, prob_ref, x_ref, *rest, away):
    hid = hid_ref.shape[0] // 2
    first = hid if away else 0
    scaled = (prob_ref[:, 0:1].astype(F32) * y_ref[...].astype(F32)).astype(BF16)
    sides = ((dg_ref, x_ref[...]), (du_ref, x_ref[...]), (hid_ref, scaled))
    for i, (left, right) in enumerate(sides):
        total = dot(left[first : first + hid, :], right)
        if away:
            rest[0][i * hid : (i + 1) * hid, :] = total.astype(BF16)
        else:
            came = rest[0][i * hid : (i + 1) * hid, :].astype(F32)
            rest[1 + i][...] = (total + came).astype(BF16)


def summed(refs):
    total = refs[0][...].astype(F32)
    for r in refs[1:]:
        total = total + r[...].astype(F32)
    return total


def join_kernel(*refs, width):
    *parts, out_ref = refs
    body = [p.at[:, pl.ds(0, width)] for p in parts]
    out_ref[:, 0:width] = summed(body).astype(BF16)
    tail = summed([p.at[:, pl.ds(width, LANES)] for p in parts])
    value = tail[:, 0:1] + tail[:, LANES // 2 : LANES // 2 + 1]
    high = value.astype(BF16).astype(F32)
    out_ref[:, width:] = jnp.where(
        iota(tail.shape, 1) < LANES // 2, high, value - high
    ).astype(BF16)


def last_kernel(*refs, group):
    *parts, out_ref = refs
    width = QN * group
    row, col = iota((LANES, LANES), 0), iota((LANES, LANES), 1)
    swap = jnp.where((col & 15) * QN + (col >> 4) == row, 1.0, 0.0).astype(BF16)
    total = summed([p.at[:, pl.ds(0, width)] for p in parts]).astype(BF16)
    for s in range(CAP):
        stack = jnp.concatenate(
            [total[s * 16 : (s + 1) * 16, k * group : (k + 1) * group] for k in range(QN)], axis=0
        )
        out_ref[:, s * group : (s + 1) * group] = dot(swap, stack).astype(BF16)
    tail = summed([p.at[:, pl.ds(width, LANES)] for p in parts])
    value = tail[:, 0:1] + tail[:, LANES // 2 : LANES // 2 + 1]
    lane = iota((16, LANES), 1)
    cols = jnp.zeros((16, LANES), F32)
    for s in range(CAP):
        cols = cols + jnp.where(lane == s, value[s * 16 : (s + 1) * 16, :], 0.0)
    stack = jnp.concatenate([cols] * QN, axis=0).astype(BF16)
    out_ref[:, CAP * group :] = dot(swap, stack).astype(BF16)


def final_kernel(ids_ref, in_ref, tok_ref, gate_ref, *, group):
    ids_t = ids_ref[...]
    live = live_tables(ids_t)
    lane = iota(live[0].shape, 1)
    sides = [jnp.transpose(v) for v in live]
    for k in range(QN):
        total = jnp.zeros((live[0].shape[1], group), F32)
        for s in range(CAP):
            pick = jnp.where((lane & (QN - 1)) == k, sides[s], 0.0).astype(BF16)
            total = total + dot(pick, in_ref[:, s * group : (s + 1) * group])
        tok_ref[:, k * group : (k + 1) * group] = total.astype(BF16)
    row = iota(live[0].shape, 0)
    value = jnp.zeros(live[0].shape, F32)
    for s in range(CAP):
        col = in_ref[:, CAP * group + s : CAP * group + s + 1].astype(F32)
        value = value + live[s] * col
    value = jnp.where((row & (QN - 1)) == 0, value, 0.0)
    for r in range(ids_t.shape[0]):
        mine = jnp.where(ids_t[r : r + 1, :] == (row >> 3), value, 0.0)
        gate_ref[r : r + 1, :] = jnp.sum(mine, axis=0, keepdims=True).astype(BF16)


def per_device(tokens, cotangent, gate_probs, expert_ids, w_gate, w_up, w_down):
    width = tokens.shape[1]
    group = width // QN
    wide = width + LANES
    rows = CAP * 16
    total = 8 * rows
    g, u, d = w_gate[0], w_up[0], w_down[0]
    hid = g.shape[0]
    ids_t, probs_t = expert_ids.T, gate_probs.T
    shape = jax.ShapeDtypeStruct
    any_spec, vmem = pl.BlockSpec(memory_space=pl.ANY), pl.BlockSpec(memory_space=pltpu.VMEM)
    dma = pltpu.SemaphoreType.DMA
    together = lax.optimization_barrier
    work = 2 * total * width * 2 * hid

    def exchange(a):
        a = a.reshape(16, QN, a.shape[1])
        a = lax.all_to_all(a, "ep", split_axis=0, concat_axis=0, tiled=True)
        return a.reshape(LANES, a.shape[2])

    def unpack(a, columns, name):
        return call(
            functools.partial(unpack_kernel, group=group),
            shape((rows, columns), BF16),
            name,
            cost=(10**8, 10**6),
        )(a)

    send_x = call(
        functools.partial(send_kernel, with_p=False),
        shape((LANES, CAP * group), BF16),
        "send_x",
        cost=(6 * 10**8, 2 * 10**6),
    )(ids_t, tokens)
    core_g, core_u, core_d = hop(g, C_SWAP), hop(u, C_SWAP), hop(d, C_SWAP)
    got_x, core_g, core_u, core_d = together((exchange(send_x), core_g, core_u, core_d))
    x = unpack(got_x, width, "unpack_x")
    xa, xb, oth = hop(x, X_A), hop(x, X_B), hop(x, Z_SWAP)
    send_y = call(
        functools.partial(send_kernel, with_p=True),
        shape((LANES, CAP * group + LANES), BF16),
        "send_y",
        cost=(6 * 10**8, 2 * 10**6),
    )(ids_t, probs_t, cotangent)
    send_y, x_now = together((send_y, x))
    got_y = exchange(send_y)
    xa, xb, oth = together((xa, xb, oth))
    ob, oa, far = hop(oth, X_B), hop(oth, X_A), hop(xa, X_A)
    o_far = hop(ob, X_B)
    far, oa, ob, got_y = together((far, oa, ob, got_y))
    y = unpack(got_y, wide, "unpack_y")
    ya, yb, y_oth = hop(y, X_A), hop(y, X_B), hop(y, Z_SWAP)
    ya, yb, y_oth = together((ya, yb, y_oth))
    yob, yoa, y_far = hop(y_oth, X_B), hop(ya, Z_SWAP), hop(ya, X_A)
    yo_far = hop(yob, X_B)
    gate, up, x_all = call(
        pre_kernel,
        [shape((2 * hid, total), F32)] * 2 + [shape((total, width), BF16)],
        "pre",
        scratch=[pltpu.VMEM((4 * hid, width), BF16), dma((32,)), dma((16,))],
        specs=[any_spec] * 12,
        cost=(2 * work, 10 * 10**6),
    )(x, xa, far, xb, oth, oa, o_far, ob, g, core_g, u, core_u)
    *parts, d_gate, d_up, hidden, y_all = call(
        main_kernel,
        [shape((rows, wide), BF16)] * 8
        + [shape((2 * hid, total), BF16)] * 3
        + [shape((total, wide), BF16)],
        "main",
        scratch=[
            pltpu.VMEM((2 * hid, width), BF16),
            pltpu.VMEM((4 * hid, width), BF16),
            pltpu.VMEM((2 * hid, total), F32),
            dma((32,)),
            dma((8,)),
            dma((16,)),
        ],
        specs=[any_spec] * 14 + [vmem] * 2,
        cost=(3 * work, 14 * 10**6),
    )(
        *(y, ya, y_far, yb, y_oth, yoa, yo_far, yob),
        *(d, core_d, g, core_g, u, core_u, gate, up),
    )

    blocks = 4

    def wgrad(*came):
        cols = width // blocks

        def part(height):
            return pl.BlockSpec((height, cols), lambda n: (0, n))

        prob = pl.BlockSpec((total, LANES), lambda n: (0, width // LANES))
        left = pl.BlockSpec((2 * hid, total), lambda n: (0, 0))
        out = [shape((hid, width), BF16)] * 3 if came else shape((3 * hid, width), BF16)
        return pl.pallas_call(
            functools.partial(wgrad_kernel, away=not came),
            out_shape=out,
            grid=(blocks,),
            in_specs=[left] * 3
            + [part(total), prob, part(total)]
            + [part(3 * hid)] * len(came),
            out_specs=[part(hid)] * 3 if came else part(3 * hid),
            compiler_params=pltpu.CompilerParams(vmem_limit_bytes=32 * 1024 * 1024),
            name="wgrad_mine" if came else "wgrad_away",
            cost_estimate=pl.CostEstimate(
                flops=work * 3 // 2, bytes_accessed=12 * 10**6, transcendentals=0
            ),
        )(hidden, d_gate, d_up, y_all, y_all, x_all, *came)

    def join(*a):
        return call(
            functools.partial(join_kernel, width=width),
            shape((rows, wide), BF16),
            "join",
            cost=(10**6, 10**6),
        )(*a)

    own, pa, far, pb, oth, oa, o_far, ob = parts
    of, oa, ob = hop(o_far, Z_SWAP), hop(oa, X_B), hop(ob, X_A)
    away = wgrad()
    of, oa, ob, pb, away = together((of, oa, ob, pb, away))
    f, oz = hop(join(far, of), X_B), hop(join(oth, oa, ob), Z_SWAP)
    pb = hop(pb, X_A)
    f, oz, pb, away = together((f, oz, pb, away))
    pa = hop(join(pa, f), X_B)
    last = call(
        functools.partial(last_kernel, group=group),
        shape((LANES, CAP * group + LANES), BF16),
        "last",
        cost=(10**8, 3 * 10**6),
    )(own, pa, pb, oz)
    last, hidden, away = together((last, hidden, away))
    came = hop(away, C_SWAP)
    back = exchange(last)
    g_grad, u_grad, d_grad = wgrad(came)
    back, g_grad, u_grad, d_grad = together((back, g_grad, u_grad, d_grad))
    token_grad, gate_t = call(
        functools.partial(final_kernel, group=group),
        [shape(tokens.shape, BF16), shape(ids_t.shape, BF16)],
        "final",
        cost=(6 * 10**8, 2 * 10**6),
    )(ids_t, back)
    return (token_grad, gate_t.T, g_grad[None], u_grad[None], d_grad[None])


def solution(mesh):
    tok = P(("edp", "ep"), None)
    wgt = P("ep", "edp", None)
    return jax.shard_map(
        per_device,
        mesh=mesh,
        in_specs=(tok, tok, tok, tok, wgt, wgt, wgt),
        out_specs=(tok, tok, wgt, wgt, wgt),
        check_vma=False,
    )
```
